512 devices in a mesh: node: 32 (over z, core), local: 16 (over y, x).
Axes of the slice: x: 4, y: 4, z: 16, core: 2. Of those that a mesh axis runs over, the one named last changes fastest.
Arguments:
- images: float32 [4096, 7, 7, 512], P(('node', 'local')), may hold values from -11 to 11, as said below
- targets: float32 [4096, 7, 7, 512], P(('node', 'local')), may hold values from -6 to 6
- weight: float32 [3, 3, 512, 512], replicated, may hold values from -0.09375 to 0.09375
Outputs:
- combined: float32 [4608, 512], P('local', 'node')
The draws below stay inside these ranges and needn't reach their ends.
Inputs may be any that keep to these rules, and one draw needn't show every extreme that they name: `images`: entries are real-valued, of order one.
All inputs are finite; a program needn't handle non-finite values.
Results may differ from the reference program's by a relative error of at most 0.00013.
Values sent between devices are 32-bit elements; how exact they have to be, the bound alone decides.
A program may use at most 128 MiB of HBM per device.

```python
import jax
import jax.numpy as jnp
from jax import lax

C = 512
SIDE = 7
IMG_DEV = 8
IMAGES = 4096
N_NODE = 32
N_LOCAL = 16


def draw_images(key, part):
    key_base, key_jitter = jax.random.split(jax.random.fold_in(key, 7101), 2)
    shape = (IMAGES, SIDE, SIDE, C)
    base = jnp.clip(jax.random.normal(key_base, shape, jnp.float32), -5.0, 5.0)
    position = jnp.arange(IMAGES, dtype=jnp.float32) / max(IMAGES - 1, 1)
    rising = jnp.exp((position - 0.5) * jnp.log(3.0))
    jitter = jnp.exp(jax.random.uniform(key_jitter, (IMAGES,), jnp.float32, jnp.log(0.8), jnp.log(1.25)))
    factor = (rising * jitter)[:, None, None, None]
    return (base * factor).astype(jnp.float32)


def block_levels(stream_key, dims, shards, low, top_value):
    level, own = 1.0, jax.random.fold_in(stream_key, 6)
    for dim, shards_of in shards:
        steps = jnp.exp(jax.random.uniform(jax.random.fold_in(own, dim), (shards_of,), jnp.float32, low / len(shards), top_value / len(shards)))
        level = level * jnp.repeat(steps, dims[dim] // shards_of).reshape([-1 if axis == dim else 1 for axis in range(len(dims))])
    return level


def noise(own_key, extent, spread, most, cuts=(), kind=jnp.bfloat16):
    loudness = block_levels(own_key, extent, cuts, -0.22, 0.18) if cuts else 1.0
    entries = jax.random.normal(own_key, extent, jnp.float32) * spread * loudness
    return jnp.minimum(jnp.maximum(entries, -most), most).astype(kind)


def setup_inputs(seed: int = 0) -> dict:
    splits = jax.random.split(jax.random.key(seed), 4)
    images = draw_images(jax.random.fold_in(splits[3], 71), 0)
    targets = noise(splits[1], (IMAGES, SIDE, SIDE, C), 1.0, 6.0, ((0, 512),), jnp.float32)
    weight = noise(splits[2], (3, 3, C, C), (9 * C) ** -0.5, 0.09375, (), jnp.float32)
    return dict(images=images, targets=targets, weight=weight)


epsilon = 1e-6


def make_patches(images):
    padded = jnp.pad(images, ((0, 0), (1, 1), (1, 1), (0, 0)))
    tap_views = []
    for row_shift in range(3):
        for col_shift in range(3):
            tap_views.append(padded[:, row_shift:row_shift + SIDE, col_shift:col_shift + SIDE, :])
    joined = jnp.concatenate(tap_views, axis=-1)
    return joined.reshape(-1, 9 * images.shape[3])


def reference(images, targets, weight):
    flat_w = weight.reshape(9 * C, C)
    node_images = images.reshape(N_NODE, N_LOCAL * IMG_DEV, SIDE, SIDE, C)
    node_targets = targets.reshape(N_NODE, N_LOCAL * IMG_DEV * SIDE * SIDE, C)

    def per_node(pair):
        patches = make_patches(pair[0])
        outputs = jnp.dot(patches, flat_w, precision=lax.Precision.HIGHEST, preferred_element_type=jnp.float32)
        residual = outputs - pair[1]
        gradient = lax.dot_general(patches, residual, (((0,), (0,)), ((), ())), precision=lax.Precision.HIGHEST, preferred_element_type=jnp.float32)
        return gradient * (1.0 / (IMG_DEV * SIDE * SIDE))

    grads = lax.map(per_node, (node_images, node_targets))
    node_ids = jnp.arange(N_NODE, dtype=jnp.int32)
    levels = N_NODE.bit_length() - 1
    for tree_level in range(levels):
        partner_ids = jnp.bitwise_xor(node_ids, jnp.int32(1 << tree_level))
        partner_grads = grads[partner_ids]
        is_upper = (jnp.bitwise_and(jnp.right_shift(node_ids, tree_level), 1) == 1)[:, None, None]
        left_vec = jnp.where(is_upper, partner_grads, grads)
        right_vec = jnp.where(is_upper, grads, partner_grads)
        cross_sum = jnp.sum(left_vec * right_vec, axis=(1, 2), keepdims=True)
        left_sq = jnp.sum(left_vec * left_vec, axis=(1, 2), keepdims=True)
        right_sq = jnp.sum(right_vec * right_vec, axis=(1, 2), keepdims=True)
        grads = (1.0 - cross_sum / (2.0 * (left_sq + epsilon))) * left_vec + (1.0 - cross_sum / (2.0 * (right_sq + epsilon))) * right_vec
    return grads[0]
```

```python
import jax
import jax.numpy as jnp
from jax import lax
from jax.sharding import PartitionSpec as P

SIDE = 7
EPS = 1e-06
HIGHEST = lax.Precision.HIGHEST


def make_patches(images):
    padded = jnp.pad(images, ((0, 0), (1, 1), (1, 1), (0, 0)))
    views = []
    for i in range(3):
        for j in range(3):
            views.append(padded[:, i : i + SIDE, j : j + SIDE, :])
    return jnp.concatenate(views, axis=-1).reshape(-1, 9 * images.shape[3])


def tree_coefs(gram):
    rows = jnp.eye(gram.shape[0], dtype=jnp.float32)
    while rows.shape[0] > 1:
        a, b = rows[0::2], rows[1::2]
        ga = jnp.dot(a, gram, precision=HIGHEST)
        gb = jnp.dot(b, gram, precision=HIGHEST)
        ab = jnp.sum(ga * b, axis=1, keepdims=True)
        aa = jnp.maximum(jnp.sum(ga * a, axis=1, keepdims=True), 0.0)
        bb = jnp.maximum(jnp.sum(gb * b, axis=1, keepdims=True), 0.0)
        rows = (1.0 - ab / (2.0 * (aa + EPS))) * a + (1.0 - ab / (2.0 * (bb + EPS))) * b
    return rows[0]


def on_device(images, targets, weight):
    channels = images.shape[3]
    nodes = lax.axis_size("node")
    flat_w = weight.reshape(9 * channels, channels)
    patches = make_patches(images)
    outputs = jnp.dot(patches, flat_w, precision=lax.Precision.HIGH, preferred_element_type=jnp.float32)
    residual = outputs - targets.reshape(-1, channels)
    product = lax.dot_general(
        patches, residual, (((0,), (0,)), ((), ())), precision=lax.Precision.HIGH, preferred_element_type=jnp.float32
    )
    mine = lax.psum_scatter(product * (1.0 / patches.shape[0]), "local", scatter_dimension=0, tiled=True)
    split = jnp.swapaxes(mine.reshape(-1, nodes, channels // nodes), 0, 1)
    blocks = lax.all_to_all(split, "node", 0, 0, tiled=True)
    flat = blocks.reshape(nodes, -1)
    gram = lax.psum(lax.dot_general(flat, flat, (((1,), (1,)), ((), ())), precision=HIGHEST), ("node", "local"))
    coefs = tree_coefs(gram)
    return jnp.sum(coefs[:, None, None] * blocks, axis=0)


def solution(mesh):
    image_spec = P(("node", "local"), None, None, None)
    return jax.shard_map(
        on_device, mesh=mesh, in_specs=(image_spec, image_spec, P()), out_specs=P("local", "node"), check_vma=False
    )
```

```python
import jax
import jax.numpy as jnp
from jax import lax
from jax.experimental import pallas as pl
from jax.experimental.pallas import tpu as pltpu
from jax.sharding import PartitionSpec as P

F32, BF16 = jnp.float32, jnp.bfloat16
EPS = 1e-06
SIDE, IMG, C, TAPS = 7, 8, 512, 9
N_NODE, N_LOCAL, RING = 32, 16, 4
ROWS_L = TAPS * C // N_LOCAL
HALF = C // 2
GRID = 8 * IMG
PAD_ROWS = 10 * GRID + 2 * IMG
OUT_ROWS = SIDE * GRID
CHUNKS = ((256, 32), (0, 64), (64, 64), (128, 64), (192, 64))
NQ = len(CHUNKS)
BASE = (0, 32, 96, 160, 224)
MESH = pl.DeviceIdType.MESH


def split(value):
    hi = value.astype(BF16)
    return hi, (value - hi.astype(F32)).astype(BF16)


def dot(a, b):
    return jnp.dot(a, b, preferred_element_type=F32)


def kernel(
    x_hbm, t_hbm, w_hbm, out_ref,
    xin, tin, wbuf, xs_hi, xs_lo, xt_hi, xt_lo, acc, r_hi, r_lo, g, p1, p2, zs, zr, gram, sb, s1, s2, s3,
    in_sem, p1_send, p1_recv, p2_send, p2_recv, z_send, z_recv, s_send, s_recv,
):
    node, local = lax.axis_index("node"), lax.axis_index("local")
    y, x = local // RING, lax.rem(local, RING)

    def at(yy, xx):
        return lax.rem(yy + RING, RING) * RING + lax.rem(xx + RING, RING)

    neighbours = ((at(y, x + 1), at(y, x - 1)), (at(y + 1, x), at(y - 1, x)))

    x_copy = pltpu.make_async_copy(x_hbm, xin, in_sem.at[0])
    t_copy = pltpu.make_async_copy(t_hbm, tin, in_sem.at[1])
    x_copy.start()
    for t in range(TAPS):
        pltpu.make_async_copy(w_hbm.at[t], wbuf.at[t], in_sem.at[2 + t]).start()
    t_copy.start()

    barrier = pltpu.get_barrier_semaphore()

    @pl.loop(1, N_LOCAL)
    def _(d):
        pl.semaphore_signal(barrier, inc=1, device_id={"local": lax.rem(local + d, N_LOCAL)}, device_id_type=MESH)

    @pl.loop(1, N_NODE)
    def _(d):
        pl.semaphore_signal(barrier, inc=1, device_id={"node": lax.rem(node + d, N_NODE)}, device_id_type=MESH)

    zero = jnp.zeros((2 * GRID, C), BF16)
    for ref in (xs_hi, xs_lo):
        for first in (0, PAD_ROWS):
            ref[first : first + GRID, :] = zero[:GRID]
            ref[first + 8 * GRID : first + 10 * GRID, :] = zero
            ref[first + 10 * GRID : first + PAD_ROWS, :] = zero[: 2 * IMG]
    r_hi[OUT_ROWS:, :] = zero[:GRID]
    r_lo[OUT_ROWS:, :] = zero[:GRID]
    acc[...] = jnp.zeros_like(acc)
    gram[...] = jnp.zeros_like(gram)
    x_copy.wait()
    edge = jnp.zeros((IMG, C), F32)

    @pl.loop(0, SIDE)
    def _(r):
        row = xin[r].reshape(SIDE * IMG, C)
        even = split(jnp.concatenate([edge, row], axis=0))
        odd = split(jnp.concatenate([row, edge], axis=0))
        first = pl.multiple_of((r + 1) * GRID, GRID)
        for ref, e, o in ((xs_hi, even[0], odd[0]), (xs_lo, even[1], odd[1])):
            ref[pl.ds(first, GRID), :] = e
            ref[pl.ds(pl.multiple_of(PAD_ROWS + first, 2 * IMG), GRID), :] = o

    @pl.loop(0, TAPS)
    def _(t):
        i, j = t // 3, lax.rem(t, 3)
        start = i * GRID + jnp.where(j == 1, PAD_ROWS, j * IMG)
        start = pl.multiple_of(start, 2 * IMG)
        pltpu.make_async_copy(w_hbm.at[t], wbuf.at[t], in_sem.at[2 + t]).wait()
        w_hi, w_lo = split(wbuf[t])
        x_hi = xs_hi[pl.ds(start, OUT_ROWS), :]
        x_lo = xs_lo[pl.ds(start, OUT_ROWS), :]
        acc[...] += dot(x_hi, w_hi) + dot(x_hi, w_lo) + dot(x_lo, w_hi)
        rows = pl.ds(pl.multiple_of(t * C, C), C)
        xt_hi[rows, :] = xs_hi[pl.ds(start, C), :].T
        xt_lo[rows, :] = xs_lo[pl.ds(start, C), :].T

    t_copy.wait()
    source = lax.broadcasted_iota(jnp.int32, (C, C), 0)
    place = lax.broadcasted_iota(jnp.int32, (C, C), 1)
    wanted = ((place & (HALF - 1)) >> 3) * 16 + (place >> 8) * 8 + (place & 7)
    order = jnp.where(source == wanted, 1.0, 0.0).astype(BF16)
    scale = 1.0 / (SIDE * SIDE * IMG)

    for r in range(SIDE):
        diff = (acc[r * GRID : r * GRID + SIDE * IMG, :] - tin[r].reshape(SIDE * IMG, C)) * scale
        hi, lo = split(jnp.concatenate([diff, edge], axis=0))
        r_hi[r * GRID : (r + 1) * GRID, :] = hi
        r_lo[r * GRID : (r + 1) * GRID, :] = lo
    r_hi[:OUT_ROWS, :] = dot(r_hi[:OUT_ROWS, :], order).astype(BF16)
    r_lo[:OUT_ROWS, :] = dot(r_lo[:OUT_ROWS, :], order).astype(BF16)

    pl.semaphore_wait(barrier, N_LOCAL + N_NODE - 2)

    def block(q, h, i, j0, j1):
        m = CHUNKS[q][1]
        first = 16 * BASE[q] + (4 * i + j0) * m
        return g.at[h, first : first + (j1 - j0) * m, :]

    def kept(q, h, j, u):
        m = CHUNKS[q][1]
        first = 16 * BASE[q] + j * m + u * (m // 2)
        return g.at[h, first : first + m // 2, :]

    def p1_slot(q, h, kind):
        m = CHUNKS[q][1]
        first = 12 * BASE[q] + kind * 2 * m
        return p1.at[h, first : first + 2 * m, :]

    def p2_slot(q, h, kind):
        m = CHUNKS[q][1]
        first = 3 * BASE[q] + kind * (m // 2)
        return p2.at[h, first : first + m // 2, :]

    P1_PART = ((2, 0, 2), (2, 2, 4), (1, 2, 4), (3, 0, 2), (1, 0, 2), (3, 2, 4))
    P2_PART = ((2, 0), (2, 1), (1, 1), (3, 0), (1, 0), (3, 1))

    def p1_copy(q, h, kind):
        n = (q * 2 + h) * 6 + kind
        return pltpu.make_async_remote_copy(
            src_ref=block(q, h, *P1_PART[kind]), dst_ref=p1_slot(q, h, kind),
            send_sem=p1_send.at[n], recv_sem=p1_recv.at[n],
            device_id={"local": neighbours[h][kind % 2]}, device_id_type=MESH,
        )

    def p2_copy(q, h, kind):
        n = (q * 2 + h) * 6 + kind
        return pltpu.make_async_remote_copy(
            src_ref=kept(q, h, *P2_PART[kind]), dst_ref=p2_slot(q, h, kind),
            send_sem=p2_send.at[n], recv_sem=p2_recv.at[n],
            device_id={"local": neighbours[1 - h][kind % 2]}, device_id_type=MESH,
        )

    def gradient(q, h, i):
        first, m = CHUNKS[q]
        parts_hi, parts_lo = [], []
        for j in range(RING):
            owner = at(y + j, x + i) if h == 0 else at(y + i, x + j)
            rows = pl.ds(pl.multiple_of(owner * ROWS_L + first, 32), m)
            parts_hi.append(xt_hi[rows, :])
            parts_lo.append(xt_lo[rows, :])
        a_hi = jnp.concatenate(parts_hi, axis=0)
        a_lo = jnp.concatenate(parts_lo, axis=0)
        cols = slice(h * HALF, (h + 1) * HALF)
        b_hi, b_lo = r_hi[:, cols], r_lo[:, cols]
        block(q, h, i, 0, 4)[...] = dot(a_hi, b_hi) + dot(a_hi, b_lo) + dot(a_lo, b_hi)

    def stage1(q):
        for h in range(2):
            gradient(q, h, 2)
            p1_copy(q, h, 0).start()
            p1_copy(q, h, 1).start()
        for h in range(2):
            gradient(q, h, 1)
            p1_copy(q, h, 2).start()
            gradient(q, h, 3)
            p1_copy(q, h, 3).start()
        for h in range(2):
            gradient(q, h, 0)

    def stage2(q):
        for h in range(2):
            for side in range(2):
                p1_copy(q, h, side).wait_recv()
                block(q, h, *P1_PART[4 + side])[...] += p1_slot(q, h, side)[...]
                p1_copy(q, h, 4 + side).start()

    def stage3(q):
        for h in range(2):
            for kind in (2, 3, 4, 5):
                p1_copy(q, h, kind).wait_recv()
            block(q, h, 0, 2, 4)[...] += p1_slot(q, h, 2)[...] + p1_slot(q, h, 5)[...]
            p2_copy(q, h, 0).start()
            p2_copy(q, h, 1).start()
            block(q, h, 0, 0, 2)[...] += p1_slot(q, h, 3)[...] + p1_slot(q, h, 4)[...]
            p2_copy(q, h, 2).start()
            p2_copy(q, h, 3).start()

    def stage4(q):
        for h in range(2):
            for side in range(2):
                p2_copy(q, h, side).wait_recv()
                kept(q, h, *P2_PART[4 + side])[...] += p2_slot(q, h, side)[...]
                p2_copy(q, h, 4 + side).start()

    def z_copy(q, peer):
        return pltpu.make_async_remote_copy(
            src_ref=zs.at[q, pl.ds(pl.multiple_of(peer * 8, 8), 8), :], dst_ref=zr.at[q, node],
            send_sem=z_send.at[q], recv_sem=z_recv.at[q],
            device_id={"node": peer}, device_id_type=MESH,
        )

    def stage5(q):
        m = CHUNKS[q][1]
        parts = []
        for h in range(2):
            for kind in (2, 3, 4, 5):
                p2_copy(q, h, kind).wait_recv()
            parts.append(kept(q, h, 0, 0)[...] + p2_slot(q, h, 3)[...] + p2_slot(q, h, 4)[...])
            parts.append(kept(q, h, 0, 1)[...] + p2_slot(q, h, 2)[...] + p2_slot(q, h, 5)[...])
            if m < 64:
                parts.append(jnp.zeros((64 - m, HALF), F32))
        zs[q] = jnp.concatenate(parts, axis=0).T

        @pl.loop(1, N_NODE)
        def _(d):
            z_copy(q, lax.rem(node + d, N_NODE)).start()

        zr[q, node] = zs[q, pl.ds(pl.multiple_of(node * 8, 8), 8), :]

    def wait_blocks(ref, count, sem):
        part = ref.at[pl.ds(0, count)]
        pltpu.make_async_copy(part, part, sem).wait()

    def stage6(q):
        wait_blocks(zr.at[q], N_NODE - 1, z_recv.at[q])
        wide = jnp.concatenate([zr[q, :, s, :] for s in range(8)], axis=1)
        gram[:, :N_NODE] += lax.dot_general(
            wide, wide, (((1,), (1,)), ((), ())), precision=lax.Precision.HIGHEST, preferred_element_type=F32
        )

    for step in range(NQ + 4):
        if step < NQ:
            stage1(step)
            stage2(step)
        if 0 <= step - 2 < NQ:
            stage4(step - 2)
        if 0 <= step - 1 < NQ:
            stage3(step - 1)
        if 0 <= step - 3 < NQ:
            stage5(step - 3)
        if 0 <= step - 4 < NQ:
            stage6(step - 4)

    def exchange(n, value, buf, count, slot, peer):
        sb[n] = value
        buf[slot] = value

        @pl.loop(1, count)
        def _(d):
            pltpu.make_async_remote_copy(
                src_ref=sb.at[n], dst_ref=buf.at[slot], send_sem=s_send.at[n], recv_sem=s_recv.at[n],
                device_id=peer(d), device_id_type=MESH,
            ).start()

        wait_blocks(buf, count - 1, s_recv.at[n])
        total = buf[0]
        for k in range(1, count):
            total = total + buf[k]
        return total

    packed = gram[0:8, :]
    for k in range(1, 4):
        packed = packed + pltpu.roll(gram[8 * k : 8 * k + 8, :], 32 * k, 1)
    group, member = node // 8, lax.rem(node, 8)
    packed = exchange(0, packed, s1, 8, member, lambda d: {"node": group * 8 + lax.rem(member + d, 8)})
    packed = exchange(1, packed, s2, 4, group, lambda d: {"node": lax.rem(group + d, 4) * 8 + member})
    packed = exchange(2, packed, s3, N_LOCAL, local, lambda d: {"local": lax.rem(local + d, N_LOCAL)})

    lane8 = lax.broadcasted_iota(jnp.int32, (8, 128), 1)
    pieces = []
    for k in range(4):
        turned = packed if k == 0 else pltpu.roll(packed, 128 - 32 * k, 1)
        pieces.append(jnp.where(lane8 < N_NODE, turned, 0.0))
    products = jnp.concatenate(pieces, axis=0)
    row = lax.broadcasted_iota(jnp.int32, (N_NODE, 128), 0)
    col = lax.broadcasted_iota(jnp.int32, (N_NODE, 128), 1)
    coefs = jnp.ones((N_NODE, 1), F32)
    level = 1
    while level < N_NODE:
        own = jnp.where(row == col, products, 0.0)
        cross = jnp.where(col == (row ^ level), products, 0.0)

        def weight(axis):
            square = jnp.maximum(jnp.sum(own, axis=axis, keepdims=True), 0.0)
            return 1.0 - jnp.sum(cross, axis=axis, keepdims=True) / (2.0 * (square + EPS))

        down = weight(1)
        coefs = coefs * down
        products = products * down * weight(0)
        products = products + jnp.where(
            (col & level) != 0, pltpu.roll(products, level, 1), pltpu.roll(products, 128 - level, 1)
        )
        products = products + jnp.where(
            (row & level) != 0, pltpu.roll(products, level, 0), pltpu.roll(products, N_NODE - level, 0)
        )
        level *= 2

    spread = jnp.broadcast_to(coefs, (N_NODE, 128))
    merged = []
    for q in range(NQ):
        total = spread[0:1, :] * zr[q, 0]
        for n in range(1, N_NODE):
            total = total + spread[n : n + 1, :] * zr[q, n]
        merged.append(total)
    for a in range(2):
        for q in range(NQ):
            first, m = CHUNKS[q]
            out_ref[8 * a : 8 * a + 8, first : first + m] = merged[q][:, 64 * a : 64 * a + m]

    for q in range(NQ):
        for h in range(2):
            for kind in range(6):
                p1_copy(q, h, kind).wait_send()
                p2_copy(q, h, kind).wait_send()
        wait_blocks(zr.at[q], N_NODE - 1, z_send.at[q])
    for n, (buf, count) in enumerate(((s1, 8), (s2, 4), (s3, N_LOCAL))):
        wait_blocks(buf, count - 1, s_send.at[n])


def on_device(images, targets, weight):
    any_spec = pl.BlockSpec(memory_space=pl.ANY)
    dma = pltpu.SemaphoreType.DMA
    vmem = pltpu.VMEM
    out = pl.pallas_call(
        kernel,
        out_shape=jax.ShapeDtypeStruct((C // N_NODE, ROWS_L), F32),
        in_specs=[any_spec] * 3,
        out_specs=pl.BlockSpec(memory_space=pltpu.VMEM),
        scratch_shapes=[
            vmem((SIDE, SIDE, IMG, C), F32), vmem((SIDE, SIDE, IMG, C), F32), vmem((TAPS, C, C), F32),
            vmem((2 * PAD_ROWS, C), BF16), vmem((2 * PAD_ROWS, C), BF16),
            vmem((TAPS * C, C), BF16), vmem((TAPS * C, C), BF16),
            vmem((OUT_ROWS, C), F32), vmem((C, C), BF16), vmem((C, C), BF16),
            vmem((2, 16 * ROWS_L, HALF), F32), vmem((2, 12 * ROWS_L, HALF), F32), vmem((2, 3 * ROWS_L, HALF), F32),
            vmem((NQ, HALF, 128), F32), vmem((NQ, N_NODE, 8, 128), F32),
            vmem((N_NODE, 128), F32), vmem((3, 8, 128), F32),
            vmem((8, 8, 128), F32), vmem((4, 8, 128), F32), vmem((N_LOCAL, 8, 128), F32),
            dma((2 + TAPS,)), dma((12 * NQ,)), dma((12 * NQ,)), dma((12 * NQ,)), dma((12 * NQ,)),
            dma((NQ,)), dma((NQ,)), dma((3,)), dma((3,)),
        ],
        compiler_params=pltpu.CompilerParams(collective_id=0, has_side_effects=True, vmem_limit_bytes=56 * 2**20),
        cost_estimate=pl.CostEstimate(flops=12 * 10**9, bytes_accessed=12 * 10**6, transcendentals=0),
    )(
        jnp.transpose(images, (1, 2, 0, 3)),
        jnp.transpose(targets, (1, 2, 0, 3)),
        weight.reshape(TAPS, C, C),
    )
    return out.T


def solution(mesh):
    image_spec = P(("node", "local"), None, None, None)
    return jax.shard_map(
        on_device, mesh=mesh, in_specs=(image_spec, image_spec, P()), out_specs=P("local", "node"), check_vma=False
    )
```

```python
import jax
import jax.numpy as jnp
from jax import lax
from jax.experimental import pallas as pl
from jax.experimental.pallas import tpu as pltpu
from jax.sharding import PartitionSpec as P

F32, BF16 = jnp.float32, jnp.bfloat16
EPS = 1e-06
SIDE, IMG, C, TAPS = 7, 8, 512, 9
N_NODE, N_LOCAL, RING = 32, 16, 4
ROWS_L = TAPS * C // N_LOCAL
HALF = C // 2
GRID = 8 * IMG
PAD_ROWS = 10 * GRID + 2 * IMG
OUT_ROWS = SIDE * GRID
CHUNKS = ((0, 64), (64, 64), (128, 64), (192, 64), (256, 32))
NQ = len(CHUNKS)
LAST = NQ - 1
P2_KINDS = (6, 6, 6, 6, 3)
BASE = (0, 64, 128, 192, 256)
MESH = pl.DeviceIdType.MESH


def split(value):
    hi = value.astype(BF16)
    return hi, (value - hi.astype(F32)).astype(BF16)


def dot(a, b):
    return jnp.dot(a, b, preferred_element_type=F32)


def kernel(
    x_hbm, t_hbm, w_hbm, out_ref,
    xin, tin, wbuf, xs_hi, xs_lo, xt_hi, xt_lo, acc, r_hi, r_lo, g, p1, p2, zs, zr, zs_last, zr_last, gram, sb, s1, s2, s3,
    in_sem, p1_send, p1_recv, p2_send, p2_recv, z_send, z_recv, s_send, s_recv,
):
    node, local = lax.axis_index("node"), lax.axis_index("local")
    y, x = local // RING, lax.rem(local, RING)

    def at(yy, xx):
        return lax.rem(yy + RING, RING) * RING + lax.rem(xx + RING, RING)

    neighbours = ((at(y, x + 1), at(y, x - 1), at(y, x + 2)), (at(y + 1, x), at(y - 1, x), at(y + 2, x)))

    x_copy = pltpu.make_async_copy(x_hbm, xin, in_sem.at[0])
    t_copy = pltpu.make_async_copy(t_hbm, tin, in_sem.at[1])
    x_copy.start()
    for t in range(TAPS):
        pltpu.make_async_copy(w_hbm.at[t], wbuf.at[t], in_sem.at[2 + t]).start()
    t_copy.start()

    barrier = pltpu.get_barrier_semaphore()

    @pl.loop(1, N_LOCAL)
    def _(d):
        pl.semaphore_signal(barrier, inc=1, device_id={"local": lax.rem(local + d, N_LOCAL)}, device_id_type=MESH)

    @pl.loop(1, N_NODE)
    def _(d):
        pl.semaphore_signal(barrier, inc=1, device_id={"node": lax.rem(node + d, N_NODE)}, device_id_type=MESH)

    zero = jnp.zeros((2 * GRID, C), BF16)
    for ref in (xs_hi, xs_lo):
        for first in (0, PAD_ROWS):
            ref[first : first + GRID, :] = zero[:GRID]
            ref[first + 8 * GRID : first + 10 * GRID, :] = zero
            ref[first + 10 * GRID : first + PAD_ROWS, :] = zero[: 2 * IMG]
    r_hi[OUT_ROWS:, :] = zero[:GRID]
    r_lo[OUT_ROWS:, :] = zero[:GRID]
    acc[...] = jnp.zeros_like(acc)
    gram[...] = jnp.zeros_like(gram)
    x_copy.wait()
    edge = jnp.zeros((IMG, C), F32)

    @pl.loop(0, SIDE)
    def _(r):
        row = xin[r].reshape(SIDE * IMG, C)
        even = split(jnp.concatenate([edge, row], axis=0))
        odd = split(jnp.concatenate([row, edge], axis=0))
        first = pl.multiple_of((r + 1) * GRID, GRID)
        for ref, e, o in ((xs_hi, even[0], odd[0]), (xs_lo, even[1], odd[1])):
            ref[pl.ds(first, GRID), :] = e
            ref[pl.ds(pl.multiple_of(PAD_ROWS + first, 2 * IMG), GRID), :] = o

    @pl.loop(0, 3)
    def _(i):
        total = acc[...]
        for j in range(3):
            t = 3 * i + j
            start = pl.multiple_of(i * GRID + (PAD_ROWS if j == 1 else j * IMG), 2 * IMG)
            pltpu.make_async_copy(w_hbm.at[t], wbuf.at[t], in_sem.at[2 + t]).wait()
            w_hi, w_lo = split(wbuf[t])
            x_hi = xs_hi[pl.ds(start, OUT_ROWS), :]
            x_lo = xs_lo[pl.ds(start, OUT_ROWS), :]
            total = total + (dot(x_hi, w_hi) + dot(x_hi, w_lo) + dot(x_lo, w_hi))
            rows = pl.ds(pl.multiple_of(t * C, C), C)
            xt_hi[rows, :] = xs_hi[pl.ds(start, C), :].T
            xt_lo[rows, :] = xs_lo[pl.ds(start, C), :].T
        acc[...] = total

    t_copy.wait()
    source = lax.broadcasted_iota(jnp.int32, (C, C), 0)
    place = lax.broadcasted_iota(jnp.int32, (C, C), 1)
    wanted = ((place & (HALF - 1)) >> 3) * 16 + (place >> 8) * 8 + (place & 7)
    order = jnp.where(source == wanted, 1.0, 0.0).astype(BF16)
    scale = 1.0 / (SIDE * SIDE * IMG)

    for r in range(SIDE):
        diff = (acc[r * GRID : r * GRID + SIDE * IMG, :] - tin[r].reshape(SIDE * IMG, C)) * scale
        hi, lo = split(jnp.concatenate([diff, edge], axis=0))
        r_hi[r * GRID : (r + 1) * GRID, :] = hi
        r_lo[r * GRID : (r + 1) * GRID, :] = lo
    r_hi[:OUT_ROWS, :] = dot(r_hi[:OUT_ROWS, :], order).astype(BF16)
    r_lo[:OUT_ROWS, :] = dot(r_lo[:OUT_ROWS, :], order).astype(BF16)

    def block(q, h, i, j0, j1):
        m = CHUNKS[q][1]
        first = 16 * BASE[q] + (4 * i + j0) * m
        return g.at[h, first : first + (j1 - j0) * m, :]

    def kept(q, h, j, u):
        m = CHUNKS[q][1]
        first = 16 * BASE[q] + j * m + u * (m // 2)
        return g.at[h, first : first + m // 2, :]

    def p1_slot(q, h, kind):
        m = CHUNKS[q][1]
        first = 12 * BASE[q] + kind * 2 * m
        return p1.at[h, first : first + 2 * m, :]

    def p2_slot(q, h, kind):
        m = CHUNKS[q][1]
        if q == LAST:
            return p2.at[h, 3 * BASE[q] + kind * m : 3 * BASE[q] + (kind + 1) * m, :]
        first = 3 * BASE[q] + kind * (m // 2)
        return p2.at[h, first : first + m // 2, :]

    P1_PART = ((2, 0, 2), (2, 2, 4), (1, 2, 4), (3, 0, 2), (1, 0, 2), (3, 2, 4))
    P2_PART = ((2, 0), (2, 1), (1, 1), (3, 0), (1, 0), (3, 1))

    def p1_copy(q, h, kind):
        n = (q * 2 + h) * 6 + kind
        return pltpu.make_async_remote_copy(
            src_ref=block(q, h, *P1_PART[kind]), dst_ref=p1_slot(q, h, kind),
            send_sem=p1_send.at[n], recv_sem=p1_recv.at[n],
            device_id={"local": neighbours[h][kind % 2]}, device_id_type=MESH,
        )

    def p2_copy(q, h, kind):
        n = (q * 2 + h) * 6 + kind
        if q == LAST:
            src, hop = block(q, h, 0, (1, 3, 2)[kind], (1, 3, 2)[kind] + 1), kind
        else:
            src, hop = kept(q, h, *P2_PART[kind]), kind % 2
        return pltpu.make_async_remote_copy(
            src_ref=src, dst_ref=p2_slot(q, h, kind),
            send_sem=p2_send.at[n], recv_sem=p2_recv.at[n],
            device_id={"local": neighbours[1 - h][hop]}, device_id_type=MESH,
        )

    def gradient(q, h, i):
        first, m = CHUNKS[q]
        parts_hi, parts_lo = [], []
        for j in range(RING):
            owner = at(y + j, x + i) if h == 0 else at(y + i, x + j)
            rows = pl.ds(pl.multiple_of(owner * ROWS_L + first, 32), m)
            parts_hi.append(xt_hi[rows, :])
            parts_lo.append(xt_lo[rows, :])
        a_hi = jnp.concatenate(parts_hi, axis=0)
        a_lo = jnp.concatenate(parts_lo, axis=0)
        cols = slice(h * HALF, (h + 1) * HALF)
        b_hi, b_lo = r_hi[:, cols], r_lo[:, cols]
        block(q, h, i, 0, 4)[...] = dot(a_hi, b_hi) + dot(a_hi, b_lo) + dot(a_lo, b_hi)

    def stage1(q):
        for h in range(2):
            gradient(q, h, 2)
            if q == h == 0:
                pl.semaphore_wait(barrier, N_LOCAL + N_NODE - 2)
            p1_copy(q, h, 0).start()
            p1_copy(q, h, 1).start()

    def stage1_rest(q):
        for h in range(2):
            for i in (1, 3, 0):
                gradient(q, h, i)

    def stage1_send(q):
        for h in range(2):
            p1_copy(q, h, 2).start()
            p1_copy(q, h, 3).start()

    def stage2(q):
        for h in range(2):
            for side in range(2):
                p1_copy(q, h, side).wait_recv()
                block(q, h, *P1_PART[4 + side])[...] += p1_slot(q, h, side)[...]
                p1_copy(q, h, 4 + side).start()

    def stage3(q):
        for h in range(2):
            for kind in (2, 3, 4, 5):
                p1_copy(q, h, kind).wait_recv()
            block(q, h, 0, 2, 4)[...] += p1_slot(q, h, 2)[...] + p1_slot(q, h, 5)[...]
            if q == LAST:
                block(q, h, 0, 0, 2)[...] += p1_slot(q, h, 3)[...] + p1_slot(q, h, 4)[...]
                for kind in (2, 0, 1):
                    p2_copy(q, h, kind).start()
                continue
            p2_copy(q, h, 0).start()
            p2_copy(q, h, 1).start()
            block(q, h, 0, 0, 2)[...] += p1_slot(q, h, 3)[...] + p1_slot(q, h, 4)[...]
            p2_copy(q, h, 2).start()
            p2_copy(q, h, 3).start()

    def stage4(q):
        if q == LAST:
            return
        for h in range(2):
            for side in range(2):
                p2_copy(q, h, side).wait_recv()
                kept(q, h, *P2_PART[4 + side])[...] += p2_slot(q, h, side)[...]
                p2_copy(q, h, 4 + side).start()

    def z_copy(q, peer):
        if q == LAST:
            src, dst = zs_last.at[peer], zr_last.at[node]
        else:
            src, dst = zs.at[q, pl.ds(pl.multiple_of(peer * 8, 8), 8), :], zr.at[q, node]
        return pltpu.make_async_remote_copy(
            src_ref=src, dst_ref=dst, send_sem=z_send.at[q], recv_sem=z_recv.at[q],
            device_id={"node": peer}, device_id_type=MESH,
        )

    def stage5(q):
        m = CHUNKS[q][1]
        parts = []
        for h in range(2):
            if q == LAST:
                for kind in (0, 1, 2):
                    p2_copy(q, h, kind).wait_recv()
                parts.append(
                    block(q, h, 0, 0, 1)[...] + p2_slot(q, h, 0)[...] + p2_slot(q, h, 1)[...] + p2_slot(q, h, 2)[...]
                )
                continue
            for kind in (2, 3, 4, 5):
                p2_copy(q, h, kind).wait_recv()
            parts.append(kept(q, h, 0, 0)[...] + p2_slot(q, h, 3)[...] + p2_slot(q, h, 4)[...])
            parts.append(kept(q, h, 0, 1)[...] + p2_slot(q, h, 2)[...] + p2_slot(q, h, 5)[...])
        if q == LAST:
            parts.append(jnp.zeros((64, HALF), F32))
            turned = jnp.concatenate(parts, axis=0).T
            behind = pltpu.roll(turned, 64, 1)
            zs_last[...] = turned.reshape(N_NODE, 8, 128)[:, 0:4, :] + behind.reshape(N_NODE, 8, 128)[:, 4:8, :]
        else:
            zs[q] = jnp.concatenate(parts, axis=0).T

        @pl.loop(0, N_NODE - 1)
        def _(k):
            far = N_NODE // 2 + jnp.where(lax.rem(k, 2) == 1, (k + 1) // 2, -((k + 1) // 2))
            z_copy(q, lax.rem(node + far, N_NODE)).start()

        if q == LAST:
            zr_last[node] = zs_last[node]
        else:
            zr[q, node] = zs[q, pl.ds(pl.multiple_of(node * 8, 8), 8), :]

    def wait_blocks(ref, count, sem):
        part = ref.at[pl.ds(0, count)]
        pltpu.make_async_copy(part, part, sem).wait()

    def landed(q):
        return zr_last if q == LAST else zr.at[q]

    def stage6(q):
        wait_blocks(landed(q), N_NODE - 1, z_recv.at[q])
        if q == LAST:
            wide = jnp.concatenate([zr_last[:, s, :] for s in range(4)], axis=1)
        else:
            wide = jnp.concatenate([zr[q, :, s, :] for s in range(8)], axis=1)
        gram[:, :N_NODE] += lax.dot_general(
            wide, wide, (((1,), (1,)), ((), ())), precision=lax.Precision.HIGHEST, preferred_element_type=F32
        )

    def when(stage, q):
        if 0 <= q < NQ:
            stage(q)

    for step in range(NQ + 3):
        when(stage1, step)
        when(stage5, step - 2)
        when(stage1_rest, step)
        when(stage3, step - 1)
        when(stage1_send, step)
        when(stage2, step)
        when(stage4, step - 1)
        when(stage6, step - 3)

    def exchange(n, value, buf, count, slot, peer):
        sb[n] = value
        buf[slot] = value

        @pl.loop(1, count)
        def _(d):
            pltpu.make_async_remote_copy(
                src_ref=sb.at[n], dst_ref=buf.at[slot], send_sem=s_send.at[n], recv_sem=s_recv.at[n],
                device_id=peer(d), device_id_type=MESH,
            ).start()

        wait_blocks(buf, count - 1, s_recv.at[n])
        total = buf[0]
        for k in range(1, count):
            total = total + buf[k]
        return total

    packed = gram[0:8, :]
    for k in range(1, 4):
        packed = packed + pltpu.roll(gram[8 * k : 8 * k + 8, :], 32 * k, 1)
    group, member = node // 8, lax.rem(node, 8)
    packed = exchange(0, packed, s1, 8, member, lambda d: {"node": group * 8 + lax.rem(member + d, 8)})
    packed = exchange(1, packed, s2, 4, group, lambda d: {"node": lax.rem(group + d, 4) * 8 + member})
    packed = exchange(2, packed, s3, N_LOCAL, local, lambda d: {"local": lax.rem(local + d, N_LOCAL)})

    lane8 = lax.broadcasted_iota(jnp.int32, (8, 128), 1)
    pieces = []
    for k in range(4):
        turned = packed if k == 0 else pltpu.roll(packed, 128 - 32 * k, 1)
        pieces.append(jnp.where(lane8 < N_NODE, turned, 0.0))
    products = jnp.concatenate(pieces, axis=0)
    row = lax.broadcasted_iota(jnp.int32, (N_NODE, 128), 0)
    col = lax.broadcasted_iota(jnp.int32, (N_NODE, 128), 1)
    coefs = jnp.ones((N_NODE, 1), F32)
    level = 1
    while level < N_NODE:
        own = jnp.where(row == col, products, 0.0)
        cross = jnp.where(col == (row ^ level), products, 0.0)

        def weight(axis):
            square = jnp.maximum(jnp.sum(own, axis=axis, keepdims=True), 0.0)
            return 1.0 - jnp.sum(cross, axis=axis, keepdims=True) / (2.0 * (square + EPS))

        down = weight(1)
        coefs = coefs * down
        products = products * down * weight(0)
        products = products + jnp.where(
            (col & level) != 0, pltpu.roll(products, level, 1), pltpu.roll(products, 128 - level, 1)
        )
        products = products + jnp.where(
            (row & level) != 0, pltpu.roll(products, level, 0), pltpu.roll(products, N_NODE - level, 0)
        )
        level *= 2

    spread = jnp.broadcast_to(coefs, (N_NODE, 128))
    merged = []
    for q in range(NQ):
        blocks = landed(q)
        total = spread[0:1, :] * blocks[0]
        for n in range(1, N_NODE):
            total = total + spread[n : n + 1, :] * blocks[n]
        merged.append(total)
    for a in range(2):
        for q in range(LAST):
            first, m = CHUNKS[q]
            out_ref[8 * a : 8 * a + 8, first : first + m] = merged[q][:, 64 * a : 64 * a + m]
        first, m = CHUNKS[LAST]
        for b in range(2):
            row0, lane0 = 8 * a + 4 * b, 64 * b + m * a
            out_ref[row0 : row0 + 4, first : first + m] = merged[LAST][:, lane0 : lane0 + m]

    for q in range(NQ):
        for h in range(2):
            for kind in range(6):
                p1_copy(q, h, kind).wait_send()
            for kind in range(P2_KINDS[q]):
                p2_copy(q, h, kind).wait_send()
        wait_blocks(landed(q), N_NODE - 1, z_send.at[q])
    for n, (buf, count) in enumerate(((s1, 8), (s2, 4), (s3, N_LOCAL))):
        wait_blocks(buf, count - 1, s_send.at[n])


def on_device(images, targets, weight):
    any_spec = pl.BlockSpec(memory_space=pl.ANY)
    dma = pltpu.SemaphoreType.DMA
    vmem = pltpu.VMEM
    out = pl.pallas_call(
        kernel,
        out_shape=jax.ShapeDtypeStruct((C // N_NODE, ROWS_L), F32),
        in_specs=[any_spec] * 3,
        out_specs=pl.BlockSpec(memory_space=pltpu.VMEM),
        scratch_shapes=[
            vmem((SIDE, SIDE, IMG, C), F32), vmem((SIDE, SIDE, IMG, C), F32), vmem((TAPS, C, C), F32),
            vmem((2 * PAD_ROWS, C), BF16), vmem((2 * PAD_ROWS, C), BF16),
            vmem((TAPS * C, C), BF16), vmem((TAPS * C, C), BF16),
            vmem((OUT_ROWS, C), F32), vmem((C, C), BF16), vmem((C, C), BF16),
            vmem((2, 16 * ROWS_L, HALF), F32), vmem((2, 12 * ROWS_L, HALF), F32), vmem((2, 3 * ROWS_L, HALF), F32),
            vmem((LAST, HALF, 128), F32), vmem((LAST, N_NODE, 8, 128), F32),
            vmem((N_NODE, 4, 128), F32), vmem((N_NODE, 4, 128), F32),
            vmem((N_NODE, 128), F32), vmem((3, 8, 128), F32),
            vmem((8, 8, 128), F32), vmem((4, 8, 128), F32), vmem((N_LOCAL, 8, 128), F32),
            dma((2 + TAPS,)), dma((12 * NQ,)), dma((12 * NQ,)), dma((12 * NQ,)), dma((12 * NQ,)),
            dma((NQ,)), dma((NQ,)), dma((3,)), dma((3,)),
        ],
        compiler_params=pltpu.CompilerParams(collective_id=0, has_side_effects=True, vmem_limit_bytes=56 * 2**20),
        cost_estimate=pl.CostEstimate(flops=12 * 10**9, bytes_accessed=12 * 10**6, transcendentals=0),
    )(
        jnp.transpose(images, (1, 2, 0, 3)),
        jnp.transpose(targets, (1, 2, 0, 3)),
        weight.reshape(TAPS, C, C),
    )
    return out.T


def solution(mesh):
    image_spec = P(("node", "local"), None, None, None)
    return jax.shard_map(
        on_device, mesh=mesh, in_specs=(image_spec, image_spec, P()), out_specs=P("local", "node"), check_vma=False
    )
```

```python
import jax
import jax.numpy as jnp
from jax import lax
from jax.experimental import pallas as pl
from jax.experimental.pallas import tpu as pltpu
from jax.sharding import PartitionSpec as P

F32, BF16 = jnp.float32, jnp.bfloat16
EPS = 1e-06
SIDE, IMG, C, TAPS = 7, 8, 512, 9
N_NODE, N_LOCAL, RING = 32, 16, 4
ROWS_L = TAPS * C // N_LOCAL
HALF = C // 2
GRID = 8 * IMG
PAD_ROWS = 10 * GRID + 2 * IMG
OUT_ROWS = SIDE * GRID
CHUNKS = ((0, 64), (64, 64), (128, 64), (192, 64), (256, 32))
NQ = len(CHUNKS)
LAST = NQ - 1
DIRECT = LAST - 1
BASE = (0, 64, 128, 192, 256)
MESH = pl.DeviceIdType.MESH


def split(value):
    hi = value.astype(BF16)
    return hi, (value - hi.astype(F32)).astype(BF16)


def dot(a, b):
    return jnp.dot(a, b, preferred_element_type=F32)


def kernel(
    x_hbm, t_hbm, w_hbm, out_ref,
    xin, tin, wbuf, xs_hi, xs_lo, xt_hi, xt_lo, acc, r_hi, r_lo, g, p1, p2, zs, zr, zs_last, zr_last, gram, sb, s1, s2, s3,
    in_sem, p1_send, p1_recv, p2_send, p2_recv, z_send, z_recv, s_send, s_recv,
):
    node, local = lax.axis_index("node"), lax.axis_index("local")
    y, x = local // RING, lax.rem(local, RING)

    def at(yy, xx):
        return lax.rem(yy + RING, RING) * RING + lax.rem(xx + RING, RING)

    neighbours = ((at(y, x + 1), at(y, x - 1), at(y, x + 2)), (at(y + 1, x), at(y - 1, x), at(y + 2, x)))

    x_copy = pltpu.make_async_copy(x_hbm, xin, in_sem.at[0])
    t_copy = pltpu.make_async_copy(t_hbm, tin, in_sem.at[1])
    x_copy.start()
    for t in range(TAPS):
        pltpu.make_async_copy(w_hbm.at[t], wbuf.at[t], in_sem.at[2 + t]).start()
    t_copy.start()

    barrier = pltpu.get_barrier_semaphore()

    @pl.loop(1, N_LOCAL)
    def _(d):
        pl.semaphore_signal(barrier, inc=1, device_id={"local": lax.rem(local + d, N_LOCAL)}, device_id_type=MESH)

    @pl.loop(1, N_NODE)
    def _(d):
        pl.semaphore_signal(barrier, inc=1, device_id={"node": lax.rem(node + d, N_NODE)}, device_id_type=MESH)

    zero = jnp.zeros((2 * GRID, C), BF16)
    for ref in (xs_hi, xs_lo):
        for first in (0, PAD_ROWS):
            ref[first : first + GRID, :] = zero[:GRID]
            ref[first + 8 * GRID : first + 10 * GRID, :] = zero
            ref[first + 10 * GRID : first + PAD_ROWS, :] = zero[: 2 * IMG]
    r_hi[OUT_ROWS:, :] = zero[:GRID]
    r_lo[OUT_ROWS:, :] = zero[:GRID]
    acc[...] = jnp.zeros_like(acc)
    gram[...] = jnp.zeros_like(gram)
    x_copy.wait()
    edge = jnp.zeros((IMG, C), F32)

    @pl.loop(0, SIDE)
    def _(r):
        row = xin[r].reshape(SIDE * IMG, C)
        even = split(jnp.concatenate([edge, row], axis=0))
        odd = split(jnp.concatenate([row, edge], axis=0))
        first = pl.multiple_of((r + 1) * GRID, GRID)
        for ref, e, o in ((xs_hi, even[0], odd[0]), (xs_lo, even[1], odd[1])):
            ref[pl.ds(first, GRID), :] = e
            ref[pl.ds(pl.multiple_of(PAD_ROWS + first, 2 * IMG), GRID), :] = o

    @pl.loop(0, 3)
    def _(i):
        total = acc[...]
        for j in range(3):
            t = 3 * i + j
            start = pl.multiple_of(i * GRID + (PAD_ROWS if j == 1 else j * IMG), 2 * IMG)
            pltpu.make_async_copy(w_hbm.at[t], wbuf.at[t], in_sem.at[2 + t]).wait()
            w_hi, w_lo = split(wbuf[t])
            x_hi = xs_hi[pl.ds(start, OUT_ROWS), :]
            x_lo = xs_lo[pl.ds(start, OUT_ROWS), :]
            total = total + (dot(x_hi, w_hi) + dot(x_hi, w_lo) + dot(x_lo, w_hi))
            rows = pl.ds(pl.multiple_of(t * C, C), C)
            xt_hi[rows, :] = xs_hi[pl.ds(start, C), :].T
            xt_lo[rows, :] = xs_lo[pl.ds(start, C), :].T
        acc[...] = total

    t_copy.wait()
    source = lax.broadcasted_iota(jnp.int32, (C, C), 0)
    place = lax.broadcasted_iota(jnp.int32, (C, C), 1)
    wanted = ((place & (HALF - 1)) >> 3) * 16 + (place >> 8) * 8 + (place & 7)
    order = jnp.where(source == wanted, 1.0, 0.0).astype(BF16)
    scale = 1.0 / (SIDE * SIDE * IMG)

    for r in range(SIDE):
        diff = (acc[r * GRID : r * GRID + SIDE * IMG, :] - tin[r].reshape(SIDE * IMG, C)) * scale
        hi, lo = split(jnp.concatenate([diff, edge], axis=0))
        r_hi[r * GRID : (r + 1) * GRID, :] = hi
        r_lo[r * GRID : (r + 1) * GRID, :] = lo
    r_hi[:OUT_ROWS, :] = dot(r_hi[:OUT_ROWS, :], order).astype(BF16)
    r_lo[:OUT_ROWS, :] = dot(r_lo[:OUT_ROWS, :], order).astype(BF16)

    def block(q, h, i, j0, j1):
        m = CHUNKS[q][1]
        first = 16 * BASE[q] + (4 * i + j0) * m
        return g.at[h, first : first + (j1 - j0) * m, :]

    def kept(q, h, j, u):
        m = CHUNKS[q][1]
        first = 16 * BASE[q] + j * m + u * (m // 2)
        return g.at[h, first : first + m // 2, :]

    def p1_slot(q, h, kind):
        m = CHUNKS[q][1]
        first = 12 * BASE[q] + kind * 2 * m
        return p1.at[h, first : first + 2 * m, :]

    def p2_slot(q, h, kind):
        m = CHUNKS[q][1]
        if q >= DIRECT:
            return p2.at[h, 3 * BASE[q] + kind * m : 3 * BASE[q] + (kind + 1) * m, :]
        first = 3 * BASE[q] + kind * (m // 2)
        return p2.at[h, first : first + m // 2, :]

    P1_PART = ((2, 0, 2), (2, 2, 4), (1, 2, 4), (3, 0, 2), (1, 0, 2), (3, 2, 4))
    P2_PART = ((2, 0), (2, 1), (1, 1), (3, 0), (1, 0), (3, 1))

    def p1_copy(q, h, kind):
        n = (q * 2 + h) * 6 + kind
        return pltpu.make_async_remote_copy(
            src_ref=block(q, h, *P1_PART[kind]), dst_ref=p1_slot(q, h, kind),
            send_sem=p1_send.at[n], recv_sem=p1_recv.at[n],
            device_id={"local": neighbours[h][kind % 2]}, device_id_type=MESH,
        )

    def p2_copy(q, h, kind):
        n = (q * 2 + h) * 6 + kind
        if q >= DIRECT:
            src, hop = block(q, h, 0, (1, 3, 2)[kind], (1, 3, 2)[kind] + 1), kind
        else:
            src, hop = kept(q, h, *P2_PART[kind]), kind % 2
        return pltpu.make_async_remote_copy(
            src_ref=src, dst_ref=p2_slot(q, h, kind),
            send_sem=p2_send.at[n], recv_sem=p2_recv.at[n],
            device_id={"local": neighbours[1 - h][hop]}, device_id_type=MESH,
        )

    def gradient(q, h, i):
        first, m = CHUNKS[q]
        parts_hi, parts_lo = [], []
        for j in range(RING):
            owner = at(y + j, x + i) if h == 0 else at(y + i, x + j)
            rows = pl.ds(pl.multiple_of(owner * ROWS_L + first, 32), m)
            parts_hi.append(xt_hi[rows, :])
            parts_lo.append(xt_lo[rows, :])
        a_hi = jnp.concatenate(parts_hi, axis=0)
        a_lo = jnp.concatenate(parts_lo, axis=0)
        cols = slice(h * HALF, (h + 1) * HALF)
        b_hi, b_lo = r_hi[:, cols], r_lo[:, cols]
        block(q, h, i, 0, 4)[...] = dot(a_hi, b_hi) + dot(a_hi, b_lo) + dot(a_lo, b_hi)

    def stage1(q):
        for h in range(2):
            gradient(q, h, 2)
            if q == h == 0:
                pl.semaphore_wait(barrier, N_LOCAL + N_NODE - 2)
            p1_copy(q, h, 0).start()
            p1_copy(q, h, 1).start()

    def stage1_rest(q):
        for h in range(2):
            for i in (1, 3, 0):
                gradient(q, h, i)

    def stage1_send(q):
        for h in range(2):
            p1_copy(q, h, 2).start()
            p1_copy(q, h, 3).start()

    def stage2(q):
        for h in range(2):
            for side in range(2):
                p1_copy(q, h, side).wait_recv()
                block(q, h, *P1_PART[4 + side])[...] += p1_slot(q, h, side)[...]
                p1_copy(q, h, 4 + side).start()

    def stage3(q):
        for h in range(2):
            for kind in (2, 3, 4, 5):
                p1_copy(q, h, kind).wait_recv()
            block(q, h, 0, 2, 4)[...] += p1_slot(q, h, 2)[...] + p1_slot(q, h, 5)[...]
            if q >= DIRECT:
                block(q, h, 0, 0, 2)[...] += p1_slot(q, h, 3)[...] + p1_slot(q, h, 4)[...]
                for kind in (2, 0, 1):
                    p2_copy(q, h, kind).start()
                continue
            p2_copy(q, h, 0).start()
            p2_copy(q, h, 1).start()
            block(q, h, 0, 0, 2)[...] += p1_slot(q, h, 3)[...] + p1_slot(q, h, 4)[...]
            p2_copy(q, h, 2).start()
            p2_copy(q, h, 3).start()

    def stage4(q):
        if q >= DIRECT:
            return
        for h in range(2):
            for side in range(2):
                p2_copy(q, h, side).wait_recv()
                kept(q, h, *P2_PART[4 + side])[...] += p2_slot(q, h, side)[...]
                p2_copy(q, h, 4 + side).start()

    def z_copy(q, peer):
        if q == LAST:
            src, dst = zs_last.at[peer], zr_last.at[node]
        else:
            src, dst = zs.at[q, pl.ds(pl.multiple_of(peer * 8, 8), 8), :], zr.at[q, node]
        return pltpu.make_async_remote_copy(
            src_ref=src, dst_ref=dst, send_sem=z_send.at[q], recv_sem=z_recv.at[q],
            device_id={"node": peer}, device_id_type=MESH,
        )

    def stage5(q):
        m = CHUNKS[q][1]
        parts = []
        for h in range(2):
            if q >= DIRECT:
                for kind in (0, 1, 2):
                    p2_copy(q, h, kind).wait_recv()
                parts.append(
                    block(q, h, 0, 0, 1)[...] + p2_slot(q, h, 0)[...] + p2_slot(q, h, 1)[...] + p2_slot(q, h, 2)[...]
                )
                continue
            for kind in (2, 3, 4, 5):
                p2_copy(q, h, kind).wait_recv()
            parts.append(kept(q, h, 0, 0)[...] + p2_slot(q, h, 3)[...] + p2_slot(q, h, 4)[...])
            parts.append(kept(q, h, 0, 1)[...] + p2_slot(q, h, 2)[...] + p2_slot(q, h, 5)[...])
        if q == LAST:
            parts.append(jnp.zeros((64, HALF), F32))
            turned = jnp.concatenate(parts, axis=0).T
            behind = pltpu.roll(turned, 64, 1)
            zs_last[...] = turned.reshape(N_NODE, 8, 128)[:, 0:4, :] + behind.reshape(N_NODE, 8, 128)[:, 4:8, :]
        else:
            zs[q] = jnp.concatenate(parts, axis=0).T

        @pl.loop(0, N_NODE - 1)
        def _(k):
            far = N_NODE // 2 + jnp.where(lax.rem(k, 2) == 1, (k + 1) // 2, -((k + 1) // 2))
            z_copy(q, lax.rem(node + far, N_NODE)).start()

        if q == LAST:
            zr_last[node] = zs_last[node]
        else:
            zr[q, node] = zs[q, pl.ds(pl.multiple_of(node * 8, 8), 8), :]

    def wait_blocks(ref, count, sem):
        part = ref.at[pl.ds(0, count)]
        pltpu.make_async_copy(part, part, sem).wait()

    def landed(q):
        return zr_last if q == LAST else zr.at[q]

    def stage6(q):
        wait_blocks(landed(q), N_NODE - 1, z_recv.at[q])
        if q == LAST:
            wide = jnp.concatenate([zr_last[:, s, :] for s in range(4)], axis=1)
        else:
            wide = jnp.concatenate([zr[q, :, s, :] for s in range(8)], axis=1)
        gram[:, :N_NODE] += lax.dot_general(
            wide, wide, (((1,), (1,)), ((), ())), precision=lax.Precision.HIGHEST, preferred_element_type=F32
        )

    def when(stage, q):
        if 0 <= q < NQ:
            stage(q)

    for step in range(NQ):
        when(stage1, step)
        when(stage5, step - 2)
        when(stage1_rest, step)
        when(stage3, step - 1)
        when(stage1_send, step)
        when(stage2, step)
        when(stage4, step - 1)
        when(stage6, step - 3)
    stage5(LAST - 1)
    stage3(LAST)
    stage6(LAST - 2)
    stage5(LAST)
    stage6(LAST - 1)
    stage6(LAST)

    def exchange(n, value, buf, count, slot, peer):
        sb[n] = value
        buf[slot] = value

        @pl.loop(1, count)
        def _(d):
            pltpu.make_async_remote_copy(
                src_ref=sb.at[n], dst_ref=buf.at[slot], send_sem=s_send.at[n], recv_sem=s_recv.at[n],
                device_id=peer(d), device_id_type=MESH,
            ).start()

        wait_blocks(buf, count - 1, s_recv.at[n])
        total = buf[0]
        for k in range(1, count):
            total = total + buf[k]
        return total

    packed = gram[0:8, :]
    for k in range(1, 4):
        packed = packed + pltpu.roll(gram[8 * k : 8 * k + 8, :], 32 * k, 1)
    group, member = node // 8, lax.rem(node, 8)
    packed = exchange(0, packed, s1, 8, member, lambda d: {"node": group * 8 + lax.rem(member + d, 8)})
    packed = exchange(1, packed, s2, 4, group, lambda d: {"node": lax.rem(group + d, 4) * 8 + member})
    packed = exchange(2, packed, s3, N_LOCAL, local, lambda d: {"local": lax.rem(local + d, N_LOCAL)})

    lane8 = lax.broadcasted_iota(jnp.int32, (8, 128), 1)
    pieces = []
    for k in range(4):
        turned = packed if k == 0 else pltpu.roll(packed, 128 - 32 * k, 1)
        pieces.append(jnp.where(lane8 < N_NODE, turned, 0.0))
    products = jnp.concatenate(pieces, axis=0)
    row = lax.broadcasted_iota(jnp.int32, (N_NODE, 128), 0)
    col = lax.broadcasted_iota(jnp.int32, (N_NODE, 128), 1)
    coefs = jnp.ones((N_NODE, 1), F32)
    level = 1
    while level < N_NODE:
        own = jnp.where(row == col, products, 0.0)
        cross = jnp.where(col == (row ^ level), products, 0.0)

        def weight(axis):
            square = jnp.maximum(jnp.sum(own, axis=axis, keepdims=True), 0.0)
            return 1.0 - jnp.sum(cross, axis=axis, keepdims=True) / (2.0 * (square + EPS))

        down = weight(1)
        coefs = coefs * down
        products = products * down * weight(0)
        products = products + jnp.where(
            (col & level) != 0, pltpu.roll(products, level, 1), pltpu.roll(products, 128 - level, 1)
        )
        products = products + jnp.where(
            (row & level) != 0, pltpu.roll(products, level, 0), pltpu.roll(products, N_NODE - level, 0)
        )
        level *= 2

    spread = jnp.broadcast_to(coefs, (N_NODE, 128))
    merged = []
    for q in range(NQ):
        blocks = landed(q)
        total = spread[0:1, :] * blocks[0]
        for n in range(1, N_NODE):
            total = total + spread[n : n + 1, :] * blocks[n]
        merged.append(total)
    for a in range(2):
        for q in range(LAST):
            first, m = CHUNKS[q]
            out_ref[8 * a : 8 * a + 8, first : first + m] = merged[q][:, 64 * a : 64 * a + m]
        first, m = CHUNKS[LAST]
        for b in range(2):
            row0, lane0 = 8 * a + 4 * b, 64 * b + m * a
            out_ref[row0 : row0 + 4, first : first + m] = merged[LAST][:, lane0 : lane0 + m]

    for q in range(NQ):
        for h in range(2):
            for kind in range(6):
                p1_copy(q, h, kind).wait_send()
            for kind in range(3 if q >= DIRECT else 6):
                p2_copy(q, h, kind).wait_send()
        wait_blocks(landed(q), N_NODE - 1, z_send.at[q])
    for n, (buf, count) in enumerate(((s1, 8), (s2, 4), (s3, N_LOCAL))):
        wait_blocks(buf, count - 1, s_send.at[n])


def on_device(images, targets, weight):
    any_spec = pl.BlockSpec(memory_space=pl.ANY)
    dma = pltpu.SemaphoreType.DMA
    vmem = pltpu.VMEM
    out = pl.pallas_call(
        kernel,
        out_shape=jax.ShapeDtypeStruct((C // N_NODE, ROWS_L), F32),
        in_specs=[any_spec] * 3,
        out_specs=pl.BlockSpec(memory_space=pltpu.VMEM),
        scratch_shapes=[
            vmem((SIDE, SIDE, IMG, C), F32), vmem((SIDE, SIDE, IMG, C), F32), vmem((TAPS, C, C), F32),
            vmem((2 * PAD_ROWS, C), BF16), vmem((2 * PAD_ROWS, C), BF16),
            vmem((TAPS * C, C), BF16), vmem((TAPS * C, C), BF16),
            vmem((OUT_ROWS, C), F32), vmem((C, C), BF16), vmem((C, C), BF16),
            vmem((2, 16 * ROWS_L, HALF), F32), vmem((2, 12 * ROWS_L, HALF), F32), vmem((2, 3 * ROWS_L, HALF), F32),
            vmem((LAST, HALF, 128), F32), vmem((LAST, N_NODE, 8, 128), F32),
            vmem((N_NODE, 4, 128), F32), vmem((N_NODE, 4, 128), F32),
            vmem((N_NODE, 128), F32), vmem((3, 8, 128), F32),
            vmem((8, 8, 128), F32), vmem((4, 8, 128), F32), vmem((N_LOCAL, 8, 128), F32),
            dma((2 + TAPS,)), dma((12 * NQ,)), dma((12 * NQ,)), dma((12 * NQ,)), dma((12 * NQ,)),
            dma((NQ,)), dma((NQ,)), dma((3,)), dma((3,)),
        ],
        compiler_params=pltpu.CompilerParams(collective_id=0, has_side_effects=True, vmem_limit_bytes=56 * 2**20),
        cost_estimate=pl.CostEstimate(flops=12 * 10**9, bytes_accessed=12 * 10**6, transcendentals=0),
    )(
        jnp.transpose(images, (1, 2, 0, 3)),
        jnp.transpose(targets, (1, 2, 0, 3)),
        weight.reshape(TAPS, C, C),
    )
    return out.T


def solution(mesh):
    image_spec = P(("node", "local"), None, None, None)
    return jax.shard_map(
        on_device, mesh=mesh, in_specs=(image_spec, image_spec, P()), out_specs=P("local", "node"), check_vma=False
    )
```

```python
import jax
import jax.numpy as jnp
from jax import lax
from jax.experimental import pallas as pl
from jax.experimental.pallas import tpu as pltpu
from jax.sharding import PartitionSpec as P

F32, BF16 = jnp.float32, jnp.bfloat16
EPS = 1e-06
SIDE, IMG, C, TAPS = 7, 8, 512, 9
N_NODE, N_LOCAL, RING = 32, 16, 4
ROWS_L = TAPS * C // N_LOCAL
HALF = C // 2
GRID = 8 * IMG
PAD_ROWS = 10 * GRID + 2 * IMG
OUT_ROWS = SIDE * GRID
CHUNKS = ((0, 64), (64, 64), (128, 64), (192, 64), (256, 32))
NQ = len(CHUNKS)
LAST = NQ - 1
DIRECT = LAST - 1
BASE = (0, 64, 128, 192, 256)
MESH = pl.DeviceIdType.MESH


def split(value):
    hi = value.astype(BF16)
    return hi, (value - hi.astype(F32)).astype(BF16)


def dot(a, b):
    return jnp.dot(a, b, preferred_element_type=F32)


def kernel(
    x_hbm, t_hbm, w_hbm, out_ref,
    xin, tin, wbuf, xs_hi, xs_lo, xt_hi, xt_lo, acc, r_hi, r_lo, g, p1, p2, zs, zr, zs_last, zr_last, gram, sb, s1, s2, s3,
    in_sem, p1_send, p1_recv, p2_send, p2_recv, z_send, z_recv, s_send, s_recv,
):
    node, local = lax.axis_index("node"), lax.axis_index("local")
    y, x = local // RING, lax.rem(local, RING)

    def at(yy, xx):
        return lax.rem(yy + RING, RING) * RING + lax.rem(xx + RING, RING)

    neighbours = ((at(y, x + 1), at(y, x - 1), at(y, x + 2)), (at(y + 1, x), at(y - 1, x), at(y + 2, x)))

    x_copy = pltpu.make_async_copy(x_hbm, xin, in_sem.at[0])
    t_copy = pltpu.make_async_copy(t_hbm, tin, in_sem.at[1])
    x_copy.start()
    for t in range(TAPS):
        pltpu.make_async_copy(w_hbm.at[t], wbuf.at[t], in_sem.at[2 + t]).start()
    t_copy.start()

    barrier = pltpu.get_barrier_semaphore()

    @pl.loop(1, N_LOCAL)
    def _(d):
        pl.semaphore_signal(barrier, inc=1, device_id={"local": lax.rem(local + d, N_LOCAL)}, device_id_type=MESH)

    @pl.loop(1, N_NODE)
    def _(d):
        pl.semaphore_signal(barrier, inc=1, device_id={"node": lax.rem(node + d, N_NODE)}, device_id_type=MESH)

    zero = jnp.zeros((2 * GRID, C), BF16)
    for ref in (xs_hi, xs_lo):
        for first in (0, PAD_ROWS):
            ref[first : first + GRID, :] = zero[:GRID]
            ref[first + 8 * GRID : first + 10 * GRID, :] = zero
            ref[first + 10 * GRID : first + PAD_ROWS, :] = zero[: 2 * IMG]
    r_hi[OUT_ROWS:, :] = zero[:GRID]
    r_lo[OUT_ROWS:, :] = zero[:GRID]
    acc[...] = jnp.zeros_like(acc)
    gram[...] = jnp.zeros_like(gram)
    x_copy.wait()
    edge = jnp.zeros((IMG, C), F32)

    @pl.loop(0, SIDE)
    def _(r):
        row = xin[r].reshape(SIDE * IMG, C)
        even = split(jnp.concatenate([edge, row], axis=0))
        odd = split(jnp.concatenate([row, edge], axis=0))
        first = pl.multiple_of((r + 1) * GRID, GRID)
        for ref, e, o in ((xs_hi, even[0], odd[0]), (xs_lo, even[1], odd[1])):
            ref[pl.ds(first, GRID), :] = e
            ref[pl.ds(pl.multiple_of(PAD_ROWS + first, 2 * IMG), GRID), :] = o

    @pl.loop(0, 3)
    def _(i):
        total = acc[...]
        for j in range(3):
            t = 3 * i + j
            start = pl.multiple_of(i * GRID + (PAD_ROWS if j == 1 else j * IMG), 2 * IMG)
            pltpu.make_async_copy(w_hbm.at[t], wbuf.at[t], in_sem.at[2 + t]).wait()
            w_hi, w_lo = split(wbuf[t])
            x_hi = xs_hi[pl.ds(start, OUT_ROWS), :]
            x_lo = xs_lo[pl.ds(start, OUT_ROWS), :]
            total = total + (dot(x_hi, w_hi) + dot(x_hi, w_lo) + dot(x_lo, w_hi))
            rows = pl.ds(pl.multiple_of(t * C, C), C)
            xt_hi[rows, :] = xs_hi[pl.ds(start, C), :].T
            xt_lo[rows, :] = xs_lo[pl.ds(start, C), :].T
        acc[...] = total

    t_copy.wait()
    source = lax.broadcasted_iota(jnp.int32, (C, C), 0)
    place = lax.broadcasted_iota(jnp.int32, (C, C), 1)
    wanted = ((place & (HALF - 1)) >> 3) * 16 + (place >> 8) * 8 + (place & 7)
    order = jnp.where(source == wanted, 1.0, 0.0).astype(BF16)
    scale = 1.0 / (SIDE * SIDE * IMG)

    for r in range(SIDE):
        diff = (acc[r * GRID : r * GRID + SIDE * IMG, :] - tin[r].reshape(SIDE * IMG, C)) * scale
        hi, lo = split(jnp.concatenate([diff, edge], axis=0))
        r_hi[r * GRID : (r + 1) * GRID, :] = hi
        r_lo[r * GRID : (r + 1) * GRID, :] = lo
    r_hi[:OUT_ROWS, :] = dot(r_hi[:OUT_ROWS, :], order).astype(BF16)
    r_lo[:OUT_ROWS, :] = dot(r_lo[:OUT_ROWS, :], order).astype(BF16)

    def block(q, h, i, j0, j1):
        m = CHUNKS[q][1]
        first = 16 * BASE[q] + (4 * i + j0) * m
        return g.at[h, first : first + (j1 - j0) * m, :]

    def kept(q, h, j, u):
        m = CHUNKS[q][1]
        first = 16 * BASE[q] + j * m + u * (m // 2)
        return g.at[h, first : first + m // 2, :]

    def p1_slot(q, h, kind):
        m = CHUNKS[q][1]
        first = 12 * BASE[q] + kind * 2 * m
        return p1.at[h, first : first + 2 * m, :]

    def p2_slot(q, h, kind):
        m = CHUNKS[q][1]
        if q >= DIRECT:
            return p2.at[h, 3 * BASE[q] + kind * m : 3 * BASE[q] + (kind + 1) * m, :]
        first = 3 * BASE[q] + kind * (m // 2)
        return p2.at[h, first : first + m // 2, :]

    P1_PART = ((2, 0, 2), (2, 2, 4), (1, 2, 4), (3, 0, 2), (1, 0, 2), (3, 2, 4))
    P2_PART = ((2, 0), (2, 1), (1, 1), (3, 0), (1, 0), (3, 1))

    def p1_copy(q, h, kind):
        n = (q * 2 + h) * 6 + kind
        return pltpu.make_async_remote_copy(
            src_ref=block(q, h, *P1_PART[kind]), dst_ref=p1_slot(q, h, kind),
            send_sem=p1_send.at[n], recv_sem=p1_recv.at[n],
            device_id={"local": neighbours[h][kind % 2]}, device_id_type=MESH,
        )

    def p2_copy(q, h, kind):
        n = (q * 2 + h) * 6 + kind
        if q >= DIRECT:
            src, hop = block(q, h, 0, (1, 3, 2)[kind], (1, 3, 2)[kind] + 1), kind
        else:
            src, hop = kept(q, h, *P2_PART[kind]), kind % 2
        return pltpu.make_async_remote_copy(
            src_ref=src, dst_ref=p2_slot(q, h, kind),
            send_sem=p2_send.at[n], recv_sem=p2_recv.at[n],
            device_id={"local": neighbours[1 - h][hop]}, device_id_type=MESH,
        )

    def gradient(q, h, i):
        first, m = CHUNKS[q]
        parts_hi, parts_lo = [], []
        for j in range(RING):
            owner = at(y + j, x + i) if h == 0 else at(y + i, x + j)
            rows = pl.ds(pl.multiple_of(owner * ROWS_L + first, 32), m)
            parts_hi.append(xt_hi[rows, :])
            parts_lo.append(xt_lo[rows, :])
        a_hi = jnp.concatenate(parts_hi, axis=0)
        a_lo = jnp.concatenate(parts_lo, axis=0)
        cols = slice(h * HALF, (h + 1) * HALF)
        b_hi, b_lo = r_hi[:, cols], r_lo[:, cols]
        block(q, h, i, 0, 4)[...] = dot(a_hi, b_hi) + dot(a_hi, b_lo) + dot(a_lo, b_hi)

    def stage1(q):
        for h in range(2):
            gradient(q, h, 2)
            if q == h == 0:
                pl.semaphore_wait(barrier, N_LOCAL + N_NODE - 2)
            p1_copy(q, h, 0).start()
            p1_copy(q, h, 1).start()

    def stage1_rest(q):
        for h in range(2):
            for i in (1, 3, 0):
                gradient(q, h, i)

    def stage1_send(q):
        for h in range(2):
            p1_copy(q, h, 2).start()
            p1_copy(q, h, 3).start()

    def stage2(q):
        for h in range(2):
            for side in range(2):
                p1_copy(q, h, side).wait_recv()
                block(q, h, *P1_PART[4 + side])[...] += p1_slot(q, h, side)[...]
                p1_copy(q, h, 4 + side).start()

    def stage3(q):
        for h in range(2):
            for kind in (2, 3, 4, 5):
                p1_copy(q, h, kind).wait_recv()
            block(q, h, 0, 2, 4)[...] += p1_slot(q, h, 2)[...] + p1_slot(q, h, 5)[...]
            if q >= DIRECT:
                block(q, h, 0, 0, 2)[...] += p1_slot(q, h, 3)[...] + p1_slot(q, h, 4)[...]
                for kind in (2, 0, 1):
                    p2_copy(q, h, kind).start()
                continue
            p2_copy(q, h, 0).start()
            p2_copy(q, h, 1).start()
            block(q, h, 0, 0, 2)[...] += p1_slot(q, h, 3)[...] + p1_slot(q, h, 4)[...]
            p2_copy(q, h, 2).start()
            p2_copy(q, h, 3).start()

    def stage4(q):
        if q >= DIRECT:
            return
        for h in range(2):
            for side in range(2):
                p2_copy(q, h, side).wait_recv()
                kept(q, h, *P2_PART[4 + side])[...] += p2_slot(q, h, side)[...]
                p2_copy(q, h, 4 + side).start()

    def z_copy(q, peer):
        if q == LAST:
            src, dst = zs_last.at[peer], zr_last.at[node]
        else:
            src, dst = zs.at[q, pl.ds(pl.multiple_of(peer * 8, 8), 8), :], zr.at[q, node]
        return pltpu.make_async_remote_copy(
            src_ref=src, dst_ref=dst, send_sem=z_send.at[q], recv_sem=z_recv.at[q],
            device_id={"node": peer}, device_id_type=MESH,
        )

    def stage5(q):
        m = CHUNKS[q][1]
        parts = []
        for h in range(2):
            if q >= DIRECT:
                for kind in (0, 1, 2):
                    p2_copy(q, h, kind).wait_recv()
                parts.append(
                    block(q, h, 0, 0, 1)[...] + p2_slot(q, h, 0)[...] + p2_slot(q, h, 1)[...] + p2_slot(q, h, 2)[...]
                )
                continue
            for kind in (2, 3, 4, 5):
                p2_copy(q, h, kind).wait_recv()
            parts.append(kept(q, h, 0, 0)[...] + p2_slot(q, h, 3)[...] + p2_slot(q, h, 4)[...])
            parts.append(kept(q, h, 0, 1)[...] + p2_slot(q, h, 2)[...] + p2_slot(q, h, 5)[...])
        if q == LAST:
            parts.append(jnp.zeros((64, HALF), F32))
            turned = jnp.concatenate(parts, axis=0).T
            behind = pltpu.roll(turned, 64, 1)
            zs_last[...] = turned.reshape(N_NODE, 8, 128)[:, 0:4, :] + behind.reshape(N_NODE, 8, 128)[:, 4:8, :]
        else:
            zs[q] = jnp.concatenate(parts, axis=0).T

        @pl.loop(0, N_NODE - 1, unroll=q == LAST)
        def _(k):
            far = N_NODE // 2 + jnp.where(lax.rem(k, 2) == 1, (k + 1) // 2, -((k + 1) // 2))
            z_copy(q, lax.rem(node + far, N_NODE)).start()

        if q == LAST:
            zr_last[node] = zs_last[node]
        else:
            zr[q, node] = zs[q, pl.ds(pl.multiple_of(node * 8, 8), 8), :]

    def wait_blocks(ref, count, sem):
        part = ref.at[pl.ds(0, count)]
        pltpu.make_async_copy(part, part, sem).wait()

    def landed(q):
        return zr_last if q == LAST else zr.at[q]

    def stage6(q):
        wait_blocks(landed(q), N_NODE - 1, z_recv.at[q])
        if q == LAST:
            wide = jnp.concatenate([zr_last[:, s, :] for s in range(4)], axis=1)
        else:
            wide = jnp.concatenate([zr[q, :, s, :] for s in range(8)], axis=1)
        gram[:, :N_NODE] += lax.dot_general(
            wide, wide, (((1,), (1,)), ((), ())), precision=lax.Precision.HIGHEST, preferred_element_type=F32
        )

    def when(stage, q):
        if 0 <= q < NQ:
            stage(q)

    for step in range(NQ):
        when(stage1, step)
        when(stage5, step - 2)
        when(stage1_rest, step)
        when(stage3, step - 1)
        when(stage1_send, step)
        when(stage2, step)
        when(stage4, step - 1)
        when(stage6, step - 3)
    stage5(LAST - 1)
    stage3(LAST)
    stage5(LAST)
    stage6(LAST - 2)
    stage6(LAST - 1)
    stage6(LAST)

    def exchange(n, value, buf, count, slot, peer):
        sb[n] = value
        buf[slot] = value

        for k in range(1, count):
            d = count // 2 + (k // 2 if k % 2 else -(k // 2))
            pltpu.make_async_remote_copy(
                src_ref=sb.at[n], dst_ref=buf.at[slot], send_sem=s_send.at[n], recv_sem=s_recv.at[n],
                device_id=peer(d), device_id_type=MESH,
            ).start()

        wait_blocks(buf, count - 1, s_recv.at[n])
        total = buf[0]
        for k in range(1, count):
            total = total + buf[k]
        return total

    packed = gram[0:8, :]
    for k in range(1, 4):
        packed = packed + pltpu.roll(gram[8 * k : 8 * k + 8, :], 32 * k, 1)
    group, member = node // 8, lax.rem(node, 8)
    packed = exchange(0, packed, s1, 8, member, lambda d: {"node": group * 8 + lax.rem(member + d, 8)})
    packed = exchange(1, packed, s2, 4, group, lambda d: {"node": lax.rem(group + d, 4) * 8 + member})
    packed = exchange(2, packed, s3, N_LOCAL, local, lambda d: {"local": lax.rem(local + d, N_LOCAL)})

    lane8 = lax.broadcasted_iota(jnp.int32, (8, 128), 1)
    pieces = []
    for k in range(4):
        turned = packed if k == 0 else pltpu.roll(packed, 128 - 32 * k, 1)
        pieces.append(jnp.where(lane8 < N_NODE, turned, 0.0))
    products = jnp.concatenate(pieces, axis=0)
    row = lax.broadcasted_iota(jnp.int32, (N_NODE, 128), 0)
    col = lax.broadcasted_iota(jnp.int32, (N_NODE, 128), 1)
    coefs = jnp.ones((N_NODE, 1), F32)
    level = 1
    while level < N_NODE:
        own = jnp.where(row == col, products, 0.0)
        cross = jnp.where(col == (row ^ level), products, 0.0)

        def weight(axis):
            square = jnp.maximum(jnp.sum(own, axis=axis, keepdims=True), 0.0)
            return 1.0 - jnp.sum(cross, axis=axis, keepdims=True) / (2.0 * (square + EPS))

        down = weight(1)
        coefs = coefs * down
        products = products * down * weight(0)
        products = products + jnp.where(
            (col & level) != 0, pltpu.roll(products, level, 1), pltpu.roll(products, 128 - level, 1)
        )
        products = products + jnp.where(
            (row & level) != 0, pltpu.roll(products, level, 0), pltpu.roll(products, N_NODE - level, 0)
        )
        level *= 2

    spread = jnp.broadcast_to(coefs, (N_NODE, 128))
    merged = []
    for q in range(NQ):
        blocks = landed(q)
        total = spread[0:1, :] * blocks[0]
        for n in range(1, N_NODE):
            total = total + spread[n : n + 1, :] * blocks[n]
        merged.append(total)
    for a in range(2):
        for q in range(LAST):
            first, m = CHUNKS[q]
            out_ref[8 * a : 8 * a + 8, first : first + m] = merged[q][:, 64 * a : 64 * a + m]
        first, m = CHUNKS[LAST]
        for b in range(2):
            row0, lane0 = 8 * a + 4 * b, 64 * b + m * a
            out_ref[row0 : row0 + 4, first : first + m] = merged[LAST][:, lane0 : lane0 + m]

    for q in range(NQ):
        for h in range(2):
            for kind in range(6):
                p1_copy(q, h, kind).wait_send()
            for kind in range(3 if q >= DIRECT else 6):
                p2_copy(q, h, kind).wait_send()
        wait_blocks(landed(q), N_NODE - 1, z_send.at[q])
    for n, (buf, count) in enumerate(((s1, 8), (s2, 4), (s3, N_LOCAL))):
        wait_blocks(buf, count - 1, s_send.at[n])


def on_device(images, targets, weight):
    any_spec = pl.BlockSpec(memory_space=pl.ANY)
    dma = pltpu.SemaphoreType.DMA
    vmem = pltpu.VMEM
    out = pl.pallas_call(
        kernel,
        out_shape=jax.ShapeDtypeStruct((C // N_NODE, ROWS_L), F32),
        in_specs=[any_spec] * 3,
        out_specs=pl.BlockSpec(memory_space=pltpu.VMEM),
        scratch_shapes=[
            vmem((SIDE, SIDE, IMG, C), F32), vmem((SIDE, SIDE, IMG, C), F32), vmem((TAPS, C, C), F32),
            vmem((2 * PAD_ROWS, C), BF16), vmem((2 * PAD_ROWS, C), BF16),
            vmem((TAPS * C, C), BF16), vmem((TAPS * C, C), BF16),
            vmem((OUT_ROWS, C), F32), vmem((C, C), BF16), vmem((C, C), BF16),
            vmem((2, 16 * ROWS_L, HALF), F32), vmem((2, 12 * ROWS_L, HALF), F32), vmem((2, 3 * ROWS_L, HALF), F32),
            vmem((LAST, HALF, 128), F32), vmem((LAST, N_NODE, 8, 128), F32),
            vmem((N_NODE, 4, 128), F32), vmem((N_NODE, 4, 128), F32),
            vmem((N_NODE, 128), F32), vmem((3, 8, 128), F32),
            vmem((8, 8, 128), F32), vmem((4, 8, 128), F32), vmem((N_LOCAL, 8, 128), F32),
            dma((2 + TAPS,)), dma((12 * NQ,)), dma((12 * NQ,)), dma((12 * NQ,)), dma((12 * NQ,)),
            dma((NQ,)), dma((NQ,)), dma((3,)), dma((3,)),
        ],
        compiler_params=pltpu.CompilerParams(collective_id=0, has_side_effects=True, vmem_limit_bytes=56 * 2**20),
        cost_estimate=pl.CostEstimate(flops=12 * 10**9, bytes_accessed=12 * 10**6, transcendentals=0),
    )(
        jnp.transpose(images, (1, 2, 0, 3)),
        jnp.transpose(targets, (1, 2, 0, 3)),
        weight.reshape(TAPS, C, C),
    )
    return out.T


def solution(mesh):
    image_spec = P(("node", "local"), None, None, None)
    return jax.shard_map(
        on_device, mesh=mesh, in_specs=(image_spec, image_spec, P()), out_specs=P("local", "node"), check_vma=False
    )
```

```python
import jax
import jax.numpy as jnp
from jax import lax
from jax.experimental import pallas as pl
from jax.experimental.pallas import tpu as pltpu
from jax.sharding import PartitionSpec as P

F32, BF16 = jnp.float32, jnp.bfloat16
EPS = 1e-06
SIDE, IMG, C, TAPS = 7, 8, 512, 9
N_NODE, N_LOCAL, RING = 32, 16, 4
ROWS_L = TAPS * C // N_LOCAL
HALF = C // 2
GRID = 8 * IMG
PAD_ROWS = 10 * GRID + 2 * IMG
OUT_ROWS = SIDE * GRID
CHUNKS = ((0, 64), (64, 64), (128, 64), (192, 64), (256, 32))
NQ = len(CHUNKS)
LAST = NQ - 1
DIRECT = LAST - 1
BASE = (0, 64, 128, 192, 256)
MESH = pl.DeviceIdType.MESH


def split(value):
    hi = value.astype(BF16)
    return hi, (value - hi.astype(F32)).astype(BF16)


def dot(a, b):
    return jnp.dot(a, b, preferred_element_type=F32)


def dot3(a_hi, a_lo, b_hi, b_lo):
    return dot(jnp.concatenate([a_hi, a_hi, a_lo], axis=1), jnp.concatenate([b_hi, b_lo, b_hi], axis=0))


def kernel(
    x_hbm, t_hbm, w_hbm, out_ref,
    xin, tin, wbuf, xs_hi, xs_lo, xt_hi, xt_lo, acc, r_hi, r_lo, g, p1, p2, zs, zr, zs_last, zr_last, gram, sb, s1, s2, s3,
    in_sem, p1_send, p1_recv, p2_send, p2_recv, z_send, z_recv, s_send, s_recv,
):
    node, local = lax.axis_index("node"), lax.axis_index("local")
    y, x = local // RING, lax.rem(local, RING)

    def at(yy, xx):
        return lax.rem(yy + RING, RING) * RING + lax.rem(xx + RING, RING)

    neighbours = ((at(y, x + 1), at(y, x - 1), at(y, x + 2)), (at(y + 1, x), at(y - 1, x), at(y + 2, x)))

    x_copy = pltpu.make_async_copy(x_hbm, xin, in_sem.at[0])
    t_copy = pltpu.make_async_copy(t_hbm, tin, in_sem.at[1])
    x_copy.start()
    for t in range(TAPS):
        pltpu.make_async_copy(w_hbm.at[t], wbuf.at[t], in_sem.at[2 + t]).start()
    t_copy.start()

    barrier = pltpu.get_barrier_semaphore()

    @pl.loop(1, N_LOCAL)
    def _(d):
        pl.semaphore_signal(barrier, inc=1, device_id={"local": lax.rem(local + d, N_LOCAL)}, device_id_type=MESH)

    @pl.loop(1, N_NODE)
    def _(d):
        pl.semaphore_signal(barrier, inc=1, device_id={"node": lax.rem(node + d, N_NODE)}, device_id_type=MESH)

    zero = jnp.zeros((2 * GRID, C), BF16)
    for ref in (xs_hi, xs_lo):
        for first in (0, PAD_ROWS):
            ref[first : first + GRID, :] = zero[:GRID]
            ref[first + 8 * GRID : first + 10 * GRID, :] = zero
            ref[first + 10 * GRID : first + PAD_ROWS, :] = zero[: 2 * IMG]
    r_hi[OUT_ROWS:, :] = zero[:GRID]
    r_lo[OUT_ROWS:, :] = zero[:GRID]
    acc[...] = jnp.zeros_like(acc)
    gram[...] = jnp.zeros_like(gram)
    x_copy.wait()
    edge = jnp.zeros((IMG, C), F32)

    @pl.loop(0, SIDE)
    def _(r):
        row = xin[r].reshape(SIDE * IMG, C)
        even = split(jnp.concatenate([edge, row], axis=0))
        odd = split(jnp.concatenate([row, edge], axis=0))
        first = pl.multiple_of((r + 1) * GRID, GRID)
        for ref, e, o in ((xs_hi, even[0], odd[0]), (xs_lo, even[1], odd[1])):
            ref[pl.ds(first, GRID), :] = e
            ref[pl.ds(pl.multiple_of(PAD_ROWS + first, 2 * IMG), GRID), :] = o

    @pl.loop(0, 3)
    def _(i):
        total = acc[...]
        for j in range(3):
            t = 3 * i + j
            start = pl.multiple_of(i * GRID + (PAD_ROWS if j == 1 else j * IMG), 2 * IMG)
            pltpu.make_async_copy(w_hbm.at[t], wbuf.at[t], in_sem.at[2 + t]).wait()
            w_hi, w_lo = split(wbuf[t])
            x_hi = xs_hi[pl.ds(start, OUT_ROWS), :]
            x_lo = xs_lo[pl.ds(start, OUT_ROWS), :]
            total = total + dot3(x_hi, x_lo, w_hi, w_lo)
            rows = pl.ds(pl.multiple_of(t * C, C), C)
            xt_hi[rows, :] = xs_hi[pl.ds(start, C), :].T
            xt_lo[rows, :] = xs_lo[pl.ds(start, C), :].T
        acc[...] = total

    t_copy.wait()
    source = lax.broadcasted_iota(jnp.int32, (C, C), 0)
    place = lax.broadcasted_iota(jnp.int32, (C, C), 1)
    wanted = ((place & (HALF - 1)) >> 3) * 16 + (place >> 8) * 8 + (place & 7)
    order = jnp.where(source == wanted, 1.0, 0.0).astype(BF16)
    scale = 1.0 / (SIDE * SIDE * IMG)

    for r in range(SIDE):
        diff = (acc[r * GRID : r * GRID + SIDE * IMG, :] - tin[r].reshape(SIDE * IMG, C)) * scale
        hi, lo = split(jnp.concatenate([diff, edge], axis=0))
        r_hi[r * GRID : (r + 1) * GRID, :] = hi
        r_lo[r * GRID : (r + 1) * GRID, :] = lo
    r_hi[:OUT_ROWS, :] = dot(r_hi[:OUT_ROWS, :], order).astype(BF16)
    r_lo[:OUT_ROWS, :] = dot(r_lo[:OUT_ROWS, :], order).astype(BF16)

    def block(q, h, i, j0, j1):
        m = CHUNKS[q][1]
        first = 16 * BASE[q] + (4 * i + j0) * m
        return g.at[h, first : first + (j1 - j0) * m, :]

    def kept(q, h, j, u):
        m = CHUNKS[q][1]
        first = 16 * BASE[q] + j * m + u * (m // 2)
        return g.at[h, first : first + m // 2, :]

    def p1_slot(q, h, kind):
        m = CHUNKS[q][1]
        first = 12 * BASE[q] + kind * 2 * m
        return p1.at[h, first : first + 2 * m, :]

    def p2_slot(q, h, kind):
        m = CHUNKS[q][1]
        if q >= DIRECT:
            return p2.at[h, 3 * BASE[q] + kind * m : 3 * BASE[q] + (kind + 1) * m, :]
        first = 3 * BASE[q] + kind * (m // 2)
        return p2.at[h, first : first + m // 2, :]

    P1_PART = ((2, 0, 2), (2, 2, 4), (1, 2, 4), (3, 0, 2), (1, 0, 2), (3, 2, 4))
    P2_PART = ((2, 0), (2, 1), (1, 1), (3, 0), (1, 0), (3, 1))

    def p1_copy(q, h, kind):
        n = (q * 2 + h) * 6 + kind
        return pltpu.make_async_remote_copy(
            src_ref=block(q, h, *P1_PART[kind]), dst_ref=p1_slot(q, h, kind),
            send_sem=p1_send.at[n], recv_sem=p1_recv.at[n],
            device_id={"local": neighbours[h][kind % 2]}, device_id_type=MESH,
        )

    def p2_copy(q, h, kind):
        n = (q * 2 + h) * 6 + kind
        if q >= DIRECT:
            src, hop = block(q, h, 0, (1, 3, 2)[kind], (1, 3, 2)[kind] + 1), kind
        else:
            src, hop = kept(q, h, *P2_PART[kind]), kind % 2
        return pltpu.make_async_remote_copy(
            src_ref=src, dst_ref=p2_slot(q, h, kind),
            send_sem=p2_send.at[n], recv_sem=p2_recv.at[n],
            device_id={"local": neighbours[1 - h][hop]}, device_id_type=MESH,
        )

    def gradient(q, h, i):
        first, m = CHUNKS[q]
        parts_hi, parts_lo = [], []
        for j in range(RING):
            owner = at(y + j, x + i) if h == 0 else at(y + i, x + j)
            rows = pl.ds(pl.multiple_of(owner * ROWS_L + first, 32), m)
            parts_hi.append(xt_hi[rows, :])
            parts_lo.append(xt_lo[rows, :])
        a_hi = jnp.concatenate(parts_hi, axis=0)
        a_lo = jnp.concatenate(parts_lo, axis=0)
        cols = slice(h * HALF, (h + 1) * HALF)
        b_hi, b_lo = r_hi[:, cols], r_lo[:, cols]
        block(q, h, i, 0, 4)[...] = dot3(a_hi, a_lo, b_hi, b_lo)

    def stage1(q):
        for h in range(2):
            gradient(q, h, 2)
            if q == h == 0:
                pl.semaphore_wait(barrier, N_LOCAL + N_NODE - 2)
            p1_copy(q, h, 0).start()
            p1_copy(q, h, 1).start()

    def stage1_rest(q):
        for h in range(2):
            for i in (1, 3, 0):
                gradient(q, h, i)

    def stage1_send(q):
        for h in range(2):
            p1_copy(q, h, 2).start()
            p1_copy(q, h, 3).start()

    def stage2(q):
        for h in range(2):
            for side in range(2):
                p1_copy(q, h, side).wait_recv()
                block(q, h, *P1_PART[4 + side])[...] += p1_slot(q, h, side)[...]
                p1_copy(q, h, 4 + side).start()

    def stage3(q):
        for h in range(2):
            for kind in (2, 3, 4, 5):
                p1_copy(q, h, kind).wait_recv()
            block(q, h, 0, 2, 4)[...] += p1_slot(q, h, 2)[...] + p1_slot(q, h, 5)[...]
            if q >= DIRECT:
                block(q, h, 0, 0, 2)[...] += p1_slot(q, h, 3)[...] + p1_slot(q, h, 4)[...]
                for kind in (2, 0, 1):
                    p2_copy(q, h, kind).start()
                continue
            p2_copy(q, h, 0).start()
            p2_copy(q, h, 1).start()
            block(q, h, 0, 0, 2)[...] += p1_slot(q, h, 3)[...] + p1_slot(q, h, 4)[...]
            p2_copy(q, h, 2).start()
            p2_copy(q, h, 3).start()

    def stage4(q):
        if q >= DIRECT:
            return
        for h in range(2):
            for side in range(2):
                p2_copy(q, h, side).wait_recv()
                kept(q, h, *P2_PART[4 + side])[...] += p2_slot(q, h, side)[...]
                p2_copy(q, h, 4 + side).start()

    def z_copy(q, peer):
        if q == LAST:
            src, dst = zs_last.at[peer], zr_last.at[node]
        else:
            src, dst = zs.at[q, pl.ds(pl.multiple_of(peer * 8, 8), 8), :], zr.at[q, node]
        return pltpu.make_async_remote_copy(
            src_ref=src, dst_ref=dst, send_sem=z_send.at[q], recv_sem=z_recv.at[q],
            device_id={"node": peer}, device_id_type=MESH,
        )

    def stage5(q):
        m = CHUNKS[q][1]
        parts = []
        for h in range(2):
            if q >= DIRECT:
                for kind in (0, 1, 2):
                    p2_copy(q, h, kind).wait_recv()
                parts.append(
                    block(q, h, 0, 0, 1)[...] + p2_slot(q, h, 0)[...] + p2_slot(q, h, 1)[...] + p2_slot(q, h, 2)[...]
                )
                continue
            for kind in (2, 3, 4, 5):
                p2_copy(q, h, kind).wait_recv()
            parts.append(kept(q, h, 0, 0)[...] + p2_slot(q, h, 3)[...] + p2_slot(q, h, 4)[...])
            parts.append(kept(q, h, 0, 1)[...] + p2_slot(q, h, 2)[...] + p2_slot(q, h, 5)[...])
        if q == LAST:
            parts.append(jnp.zeros((64, HALF), F32))
            turned = jnp.concatenate(parts, axis=0).T
            behind = pltpu.roll(turned, 64, 1)
            zs_last[...] = turned.reshape(N_NODE, 8, 128)[:, 0:4, :] + behind.reshape(N_NODE, 8, 128)[:, 4:8, :]
        else:
            zs[q] = jnp.concatenate(parts, axis=0).T

        @pl.loop(0, N_NODE - 1, unroll=q == LAST)
        def _(k):
            far = N_NODE // 2 + jnp.where(lax.rem(k, 2) == 1, (k + 1) // 2, -((k + 1) // 2))
            z_copy(q, lax.rem(node + far, N_NODE)).start()

        if q == LAST:
            zr_last[node] = zs_last[node]
        else:
            zr[q, node] = zs[q, pl.ds(pl.multiple_of(node * 8, 8), 8), :]

    def wait_blocks(ref, count, sem):
        part = ref.at[pl.ds(0, count)]
        pltpu.make_async_copy(part, part, sem).wait()

    def landed(q):
        return zr_last if q == LAST else zr.at[q]

    def stage6(q):
        wait_blocks(landed(q), N_NODE - 1, z_recv.at[q])
        if q == LAST:
            wide = jnp.concatenate([zr_last[:, s, :] for s in range(4)], axis=1)
        else:
            wide = jnp.concatenate([zr[q, :, s, :] for s in range(8)], axis=1)
        gram[:, :N_NODE] += lax.dot_general(
            wide, wide, (((1,), (1,)), ((), ())), precision=lax.Precision.HIGHEST, preferred_element_type=F32
        )

    def when(stage, q):
        if 0 <= q < NQ:
            stage(q)

    for step in range(NQ):
        when(stage1, step)
        when(stage5, step - 2)
        when(stage1_rest, step)
        when(stage3, step - 1)
        when(stage1_send, step)
        when(stage2, step)
        when(stage4, step - 1)
        when(stage6, step - 3)
    stage5(LAST - 1)
    stage3(LAST)
    stage5(LAST)
    stage6(LAST - 2)
    stage6(LAST - 1)
    stage6(LAST)

    def exchange(n, value, buf, count, slot, peer):
        sb[n] = value
        buf[slot] = value

        for k in range(1, count):
            d = count // 2 + (k // 2 if k % 2 else -(k // 2))
            pltpu.make_async_remote_copy(
                src_ref=sb.at[n], dst_ref=buf.at[slot], send_sem=s_send.at[n], recv_sem=s_recv.at[n],
                device_id=peer(d), device_id_type=MESH,
            ).start()

        wait_blocks(buf, count - 1, s_recv.at[n])
        total = buf[0]
        for k in range(1, count):
            total = total + buf[k]
        return total

    packed = gram[0:8, :]
    for k in range(1, 4):
        packed = packed + pltpu.roll(gram[8 * k : 8 * k + 8, :], 32 * k, 1)
    group, member = node // 8, lax.rem(node, 8)
    packed = exchange(0, packed, s1, 8, member, lambda d: {"node": group * 8 + lax.rem(member + d, 8)})
    packed = exchange(1, packed, s2, 4, group, lambda d: {"node": lax.rem(group + d, 4) * 8 + member})
    packed = exchange(2, packed, s3, N_LOCAL, local, lambda d: {"local": lax.rem(local + d, N_LOCAL)})

    lane8 = lax.broadcasted_iota(jnp.int32, (8, 128), 1)
    pieces = []
    for k in range(4):
        turned = packed if k == 0 else pltpu.roll(packed, 128 - 32 * k, 1)
        pieces.append(jnp.where(lane8 < N_NODE, turned, 0.0))
    products = jnp.concatenate(pieces, axis=0)
    row = lax.broadcasted_iota(jnp.int32, (N_NODE, 128), 0)
    col = lax.broadcasted_iota(jnp.int32, (N_NODE, 128), 1)
    coefs = jnp.ones((N_NODE, 1), F32)
    level = 1
    while level < N_NODE:
        own = jnp.where(row == col, products, 0.0)
        cross = jnp.where(col == (row ^ level), products, 0.0)

        def weight(axis):
            square = jnp.maximum(jnp.sum(own, axis=axis, keepdims=True), 0.0)
            return 1.0 - jnp.sum(cross, axis=axis, keepdims=True) / (2.0 * (square + EPS))

        down = weight(1)
        coefs = coefs * down
        products = products * down * weight(0)
        products = products + jnp.where(
            (col & level) != 0, pltpu.roll(products, level, 1), pltpu.roll(products, 128 - level, 1)
        )
        products = products + jnp.where(
            (row & level) != 0, pltpu.roll(products, level, 0), pltpu.roll(products, N_NODE - level, 0)
        )
        level *= 2

    spread = jnp.broadcast_to(coefs, (N_NODE, 128))
    merged = []
    for q in range(NQ):
        blocks = landed(q)
        total = spread[0:1, :] * blocks[0]
        for n in range(1, N_NODE):
            total = total + spread[n : n + 1, :] * blocks[n]
        merged.append(total)
    for a in range(2):
        for q in range(LAST):
            first, m = CHUNKS[q]
            out_ref[8 * a : 8 * a + 8, first : first + m] = merged[q][:, 64 * a : 64 * a + m]
        first, m = CHUNKS[LAST]
        for b in range(2):
            row0, lane0 = 8 * a + 4 * b, 64 * b + m * a
            out_ref[row0 : row0 + 4, first : first + m] = merged[LAST][:, lane0 : lane0 + m]

    for q in range(NQ):
        for h in range(2):
            for kind in range(6):
                p1_copy(q, h, kind).wait_send()
            for kind in range(3 if q >= DIRECT else 6):
                p2_copy(q, h, kind).wait_send()
        wait_blocks(landed(q), N_NODE - 1, z_send.at[q])
    for n, (buf, count) in enumerate(((s1, 8), (s2, 4), (s3, N_LOCAL))):
        wait_blocks(buf, count - 1, s_send.at[n])


def on_device(images, targets, weight):
    any_spec = pl.BlockSpec(memory_space=pl.ANY)
    dma = pltpu.SemaphoreType.DMA
    vmem = pltpu.VMEM
    out = pl.pallas_call(
        kernel,
        out_shape=jax.ShapeDtypeStruct((C // N_NODE, ROWS_L), F32),
        in_specs=[any_spec] * 3,
        out_specs=pl.BlockSpec(memory_space=pltpu.VMEM),
        scratch_shapes=[
            vmem((SIDE, SIDE, IMG, C), F32), vmem((SIDE, SIDE, IMG, C), F32), vmem((TAPS, C, C), F32),
            vmem((2 * PAD_ROWS, C), BF16), vmem((2 * PAD_ROWS, C), BF16),
            vmem((TAPS * C, C), BF16), vmem((TAPS * C, C), BF16),
            vmem((OUT_ROWS, C), F32), vmem((C, C), BF16), vmem((C, C), BF16),
            vmem((2, 16 * ROWS_L, HALF), F32), vmem((2, 12 * ROWS_L, HALF), F32), vmem((2, 3 * ROWS_L, HALF), F32),
            vmem((LAST, HALF, 128), F32), vmem((LAST, N_NODE, 8, 128), F32),
            vmem((N_NODE, 4, 128), F32), vmem((N_NODE, 4, 128), F32),
            vmem((N_NODE, 128), F32), vmem((3, 8, 128), F32),
            vmem((8, 8, 128), F32), vmem((4, 8, 128), F32), vmem((N_LOCAL, 8, 128), F32),
            dma((2 + TAPS,)), dma((12 * NQ,)), dma((12 * NQ,)), dma((12 * NQ,)), dma((12 * NQ,)),
            dma((NQ,)), dma((NQ,)), dma((3,)), dma((3,)),
        ],
        compiler_params=pltpu.CompilerParams(collective_id=0, has_side_effects=True, vmem_limit_bytes=56 * 2**20),
        cost_estimate=pl.CostEstimate(flops=12 * 10**9, bytes_accessed=12 * 10**6, transcendentals=0),
    )(
        jnp.transpose(images, (1, 2, 0, 3)),
        jnp.transpose(targets, (1, 2, 0, 3)),
        weight.reshape(TAPS, C, C),
    )
    return out.T


def solution(mesh):
    image_spec = P(("node", "local"), None, None, None)
    return jax.shard_map(
        on_device, mesh=mesh, in_specs=(image_spec, image_spec, P()), out_specs=P("local", "node"), check_vma=False
    )
```
